128 devices in a mesh: stream: 4 (over y), tile: 32 (over x, z, core).
Axes of the slice: x: 4, y: 4, z: 4, core: 2. Of those that a mesh axis runs over, the one named last changes fastest.
Arguments:
- concentration: bfloat16 [2, 768, 1024, 128], P(None, 'stream', 'tile'), may hold values from 0.29882812 to 3
- potential: bfloat16 [768, 1024, 128], P('stream', 'tile'), may hold values from -4 to 4
- diffusivity: bfloat16 [768, 1024, 128], P('stream', 'tile'), may hold values from 0.5 to 2
- spacer: int32 [768, 1024, 128], P('stream', 'tile'), may hold values 0 or 1
- velocity: bfloat16 [3, 768, 1024, 128], P(None, 'stream', 'tile'), may hold values from -4 to 4
- balance_plan: int32 [3072, 1], P(('stream', 'tile')), may hold values from 0 to 31; in each aligned block of 24 rows (0 to 23, 24 to 47, ...) at most 2 rows name the same one
Outputs:
- concentration_next: bfloat16 [2, 768, 1024, 128], P(None, 'stream', 'tile')
- velocity_next: bfloat16 [3, 768, 1024, 128], P(None, 'stream', 'tile')
- owned_charge: bfloat16 [8192, 32, 1024], P(('stream', 'tile'))
The draws below stay inside these ranges and needn't reach their ends.
Inputs may be any that keep to these rules, and one draw needn't show every extreme that they name: 1 marks fluid, 0 a spacer filament. `balance_plan`: the 24 blocks of one slab tile (aligned rows of one device) name owners among the 32 tiles of the same slab; at most 2 of them name the same owner, and some slab tile has exactly 2 with one owner.
All inputs are finite; a program needn't handle non-finite values. No bound on the sum of `spacer` on one device may be relied on, other than what follows from the above.
Results may differ from the reference program's by a relative error of at most 0.011.
Values may be sent and summed in bfloat16 or wider, within the bound.
A program may use at most 256 MiB of HBM per device.

```python
import math
import jax
import jax.numpy as jnp
import numpy as np
from jax import lax

BLK = 32
BX = 6
BZ = 4
BPD = 24
CAP = 2
SLOTS = 64
NX = 768
NY = 1024
NZ = 128
N_STREAM = 4
N_TILE = 32


def with_ends(array, stream_key, low, largest):
    index_at = [jax.random.randint(jax.random.fold_in(stream_key, axis), (), 0, length) for axis, length in enumerate(array.shape)]
    main_axis = array.shape.index(max(array.shape))
    neighbour = index_at[:main_axis] + [(index_at[main_axis] + 1) % array.shape[main_axis]] + index_at[main_axis + 1:]
    return array.at[tuple(index_at)].set(low).at[tuple(neighbour)].set(largest)


def block_scale(rng, dims, cuts, smallest, largest):
    factor_of, own = 1.0, jax.random.fold_in(rng, 6)
    for dim, shards_of in cuts:
        draws = jnp.exp(jax.random.uniform(jax.random.fold_in(own, dim), (shards_of,), jnp.float32, smallest / len(cuts), largest / len(cuts)))
        factor_of = factor_of * jnp.repeat(draws, dims[dim] // shards_of).reshape([-1 if axis == dim else 1 for axis in range(len(dims))])
    return factor_of


def shared_out(own_key, own, number, rows, number_of, top, reach, skew):
    sequence = jax.random.permutation(own_key, number_of)
    packed, usual = shares(number_of, rows * top, reach, skew, True), shares(number_of, rows * top, reach, skew, False)
    places = jnp.arange(number_of)

    def named(tallies, turn):
        used = int((tallies > 0).sum())
        fixed = max(1, used // 4)
        shifted = fixed + (places - fixed + turn * (used - fixed)) % max(1, number_of - fixed)
        return jnp.zeros((number_of,), jnp.int32).at[sequence[jnp.where(places < fixed, places, shifted)]].set(jnp.asarray(tallies, jnp.int32))

    tallies = jnp.where(number % 4 == 0, named(packed, number // 4), named(usual, number - number // 4 - 1))
    mixed = jax.random.permutation(jax.random.fold_in(own, 3), number_of)
    source_of, sink = mixed[0:number_of // 2 * 2:2], mixed[1:number_of // 2 * 2:2]
    margin = jnp.minimum(tallies[source_of] - 1, reach - tallies[sink]) // 2
    margin = jnp.where((source_of == sequence[0]) | (sink == sequence[0]) | (tallies[sink] == 0), 0, jnp.maximum(margin, 0))
    shifted = jax.random.randint(jax.random.fold_in(own, 4), (number_of // 2,), 0, 1 << 20) % (margin + 1)
    tallies = tallies.at[source_of].add(-shifted).at[sink].add(shifted)
    members = jnp.searchsorted(jnp.cumsum(tallies), jnp.arange(rows * top), side="right").astype(jnp.int32)
    listing = members.reshape(top, rows).T
    listing = listing[jax.random.permutation(jax.random.fold_in(own, 1), rows)]
    turn = jax.random.randint(jax.random.fold_in(own, 2), (rows, 1), 0, top)
    return jnp.take_along_axis(listing, (jnp.arange(top)[None, :] + turn) % top, axis=1)


def shares(amount, total, reach, slope, full):
    loads = [(1 << 20) // math.isqrt(grade ** slope) + 1 for grade in range(1, amount + 1)]
    largest = reach if full else min(reach, max(-(-total // amount), total * loads[0] // sum(loads)))
    least = 1 if total - largest >= amount - 1 else 0
    given, spare = [largest] + [least] * (amount - 1), total - largest - least * (amount - 1)
    while spare > 0:
        free = [i for i in range(1, amount) if given[i] < largest] or [i for i in range(1, amount) if given[i] < reach]
        pool, remaining = sum([loads[i] for i in free]), spare
        for i in free:
            extra = min(reach - given[i], max(1, remaining * loads[i] // pool), spare)
            given[i] = given[i] + extra
            spare = spare - extra
    return np.array(given)


def normal_values(stream_key, extent, width, most, shards=(), kind=jnp.bfloat16):
    values = width * jax.random.normal(stream_key, extent, jnp.float32)
    if shards:
        values = values * block_scale(stream_key, extent, shards, -0.22, 0.18)
    return jnp.clip(values, -most, most).astype(kind)


def setup_inputs(seed: int = 0) -> dict:
    seeds = jax.random.split(jax.random.key(seed), 7)
    concentration = jnp.clip(jnp.exp(math.log(3.0) - 2.306499 * jax.random.uniform(seeds[0], (2, NX, NY, NZ), jnp.float32) ** block_scale(seeds[0], (2, NX, NY, NZ), ((1, 4), (2, 32)), -0.2, 0.2)), 0.29882812, 3.0).astype(jnp.bfloat16)
    potential = normal_values(seeds[1], (NX, NY, NZ), 1.0, 4.0, ((0, 4), (1, 32)))
    diffusivity = jnp.clip(jnp.exp(math.log(2.0) - 1.3862944 * jax.random.uniform(seeds[2], (NX, NY, NZ), jnp.float32) ** block_scale(seeds[2], (NX, NY, NZ), ((0, 4), (1, 32)), -0.2, 0.2)), 0.5, 2.0).astype(jnp.bfloat16)
    spacer = with_ends((jax.random.randint(seeds[3], (NX, NY, NZ), 0, 4) < 3).astype(jnp.int32), jax.random.fold_in(seeds[3], 1), 0, 1)
    velocity = normal_values(seeds[4], (3, NX, NY, NZ), 1.0, 4.0, ((1, 4), (2, 32)))
    balance_plan_keys = jax.random.split(jax.random.fold_in(seeds[5], 1), (N_STREAM * N_TILE * BPD) // BPD)
    balance_plan_turns = jax.random.permutation(jax.random.fold_in(seeds[5], 3), (N_STREAM * N_TILE * BPD) // BPD)
    balance_plan = jax.vmap(lambda own, number: shared_out(jax.random.fold_in(seeds[5], 2), own, number, BPD, N_TILE, 1, CAP, 1))(balance_plan_keys, balance_plan_turns).reshape((N_STREAM * N_TILE * BPD, 1))
    return dict(concentration=concentration, potential=potential, diffusivity=diffusivity, spacer=spacer, velocity=velocity, balance_plan=balance_plan)


ion_step = 0.04
flow_step = 0.1
viscosity = 0.5
species_diff = (1.0, 1.5)
species_charge = (1.0, -1.0)

def neighbor_view(source, axis_number, offset):
    first = [1, 1, 1]
    first[axis_number] = 1 + offset
    return source[first[0]:first[0] + source.shape[0] - 2, first[1]:first[1] + source.shape[1] - 2, first[2]:first[2] + source.shape[2] - 2]

def interior_view(source):
    return source[1:-1, 1:-1, 1:-1]

def ion_update(padded):
    fields = padded.astype(jnp.float32)
    electric = fields[2]
    openness = fields[3]
    open_mid = interior_view(openness)
    pot_mid = interior_view(electric)
    updated = []
    for species in range(2):
        density = fields[species]
        dens_mid = interior_view(density)
        running = jnp.zeros_like(dens_mid)
        for axis_number in range(3):
            for offset in (-1, 1):
                dens_near = neighbor_view(density, axis_number, offset)
                pot_near = neighbor_view(electric, axis_number, offset)
                face_coef = jnp.sqrt(open_mid * neighbor_view(openness, axis_number, offset))
                running = running + face_coef * (dens_near - dens_mid + species_charge[species] * 0.5 * (dens_mid + dens_near) * (pot_near - pot_mid))
        updated.append(dens_mid + ion_step * species_diff[species] * running)
    return jnp.stack(updated)

def flow_update(flow_pad, pot_pad, charge, fluid_cells):
    flow_field = flow_pad.astype(jnp.float32)
    electric = pot_pad.astype(jnp.float32)
    middle = [interior_view(flow_field[component]) for component in range(3)]
    result = []
    for component in range(3):
        advect = jnp.zeros_like(middle[component])
        diffuse = -6.0 * middle[component]
        for axis_number in range(3):
            forward = neighbor_view(flow_field[component], axis_number, 1)
            backward = neighbor_view(flow_field[component], axis_number, -1)
            advect = advect + middle[axis_number] * 0.5 * (forward - backward)
            diffuse = diffuse + forward + backward
        field_part = -0.5 * (neighbor_view(electric, component, 1) - neighbor_view(electric, component, -1))
        result.append(fluid_cells * (middle[component] + flow_step * (viscosity * diffuse - advect + charge * field_part)))
    return jnp.stack(result).astype(jnp.bfloat16)

def wrap_pad(stack):
    stack = jnp.concatenate([stack[:, :, -1:], stack, stack[:, :, :1]], axis=2)
    return jnp.pad(stack, ((0, 0), (0, 0), (0, 0), (1, 1)))

def reference(concentration, potential, diffusivity, spacer, velocity, balance_plan):
    openness = jnp.where(spacer > 0, diffusivity, jnp.zeros_like(diffusivity))
    moving = jnp.where(spacer[None] > 0, velocity, jnp.zeros_like(velocity))
    slab_count = NX // BLK

    def one_slab(number):
        positions = (number * BLK - 1 + jnp.arange(BLK + 2, dtype=jnp.int32)) % NX
        ions = jnp.concatenate([jnp.take(concentration, positions, axis=1), jnp.take(potential, positions, axis=0)[None], jnp.take(openness, positions, axis=0)[None]], axis=0)
        ions = wrap_pad(ions)
        motion = wrap_pad(jnp.take(moving, positions, axis=1))
        conc_new = ion_update(ions).astype(jnp.bfloat16)
        charge = conc_new[0].astype(jnp.float32) - conc_new[1].astype(jnp.float32)
        fluid_cells = (lax.dynamic_slice_in_dim(spacer, number * BLK, BLK, 0) > 0).astype(jnp.float32)
        flow_new = flow_update(motion, ions[2], charge, fluid_cells)
        return (conc_new, charge.astype(jnp.bfloat16), flow_new)
    conc_slabs, charge_slabs, flow_slabs = lax.map(one_slab, jnp.arange(slab_count, dtype=jnp.int32))
    conc_out = conc_slabs.transpose(1, 0, 2, 3, 4).reshape(2, NX, NY, NZ)
    flow_out = flow_slabs.transpose(1, 0, 2, 3, 4).reshape(3, NX, NY, NZ)
    charge_field = charge_slabs.reshape(NX, NY, NZ)
    blocks = charge_field.reshape(N_STREAM, BX, BLK, N_TILE, BLK, BZ, BLK).transpose(0, 3, 1, 5, 2, 4, 6).reshape(N_STREAM, N_TILE, BPD, BLK, BLK * BLK)
    owners = balance_plan[:, 0].reshape(N_STREAM, N_TILE, BPD)
    same_owner = owners[:, :, :, None] == owners[:, :, None, :]
    earlier = jnp.arange(BPD, dtype=jnp.int32)[:, None] < jnp.arange(BPD, dtype=jnp.int32)[None, :]
    ranking = lax.optimization_barrier(jnp.sum(jnp.logical_and(same_owner, earlier[None, None]).astype(jnp.int32), axis=2)).astype(jnp.int32)
    slot_index = jnp.arange(N_TILE, dtype=jnp.int32)[None, :, None] * CAP + ranking
    stream_index = jnp.broadcast_to(jnp.arange(N_STREAM, dtype=jnp.int32)[:, None, None], owners.shape)
    owned = jnp.zeros((N_STREAM, N_TILE, SLOTS, BLK, BLK * BLK), jnp.bfloat16).at[stream_index, owners, slot_index].set(blocks)
    return (conc_out, flow_out, owned.reshape(N_STREAM * N_TILE * SLOTS, BLK, BLK * BLK))
```

```python
import functools

import jax
import jax.numpy as jnp
import numpy as np
from jax import lax
from jax.experimental import pallas as pl
from jax.experimental.pallas import tpu as pltpu
from jax.sharding import PartitionSpec as P

BLK = 32
BX = 6
BZ = 4
NXL = BX * BLK
NYL = BLK
NZL = BZ * BLK
ROWS = 48
LOW = 8
GROUP = 4

ion_step = 0.04
flow_step = 0.1
viscosity = 0.5
species_diff = (1.0, 1.5)

f32 = jnp.float32
bf16 = jnp.bfloat16


def near_sum_matrix():
    line = np.arange(NZL)
    return (np.abs(line[:, None] - line[None, :]) == 1).astype(np.float32)


def difference_matrix():
    line = np.arange(NZL)
    step = line[:, None] - line[None, :]
    return (step == 1).astype(np.float32) - (step == -1).astype(np.float32)


def block_order_matrix():
    order = np.zeros((4 * NZL, 4 * NZL), np.float32)
    for part in range(4):
        for block in range(BZ):
            for cell in range(BLK):
                order[part * NZL + block * BLK + cell, block * NZL + part * BLK + cell] = 1
    return order


def load_copies(pairs, sem, chunk):
    span = pl.ds(chunk * BLK, BLK)
    inner = pl.ds(chunk * BLK + 1, BLK)
    copies = []
    for number, (source, target, lead) in enumerate(pairs):
        index_from = (slice(None),) * lead + (span,)
        index_to = (slice(None),) * lead + (inner,)
        copies.append(
            pltpu.make_async_copy(source.at[index_from], target.at[index_to], sem.at[number, chunk])
        )
    return copies


def wait_chunks(step, pairs, sem):
    @pl.when(step == 0)
    def _():
        for copy in load_copies(pairs, sem, 0):
            copy.wait()

    @pl.when(step < BX - 1)
    def _():
        for copy in load_copies(pairs, sem, step + 1):
            copy.wait()


def ion_kernel(
    target_ref, filled_ref, conc_ref, pot_ref, diff_ref, spacer_ref, xlo_ref, xhi_ref,
    ylo_ref, yhi_ref, near_ref, order_ref,
    next_ref, out_ref,
    conc_in, pot_in, diff_in, spacer_in, wide, half, charge, lines, blocks, empty,
    load_sem, block_sem, empty_sem,
):
    step = pl.program_id(0)
    slots = filled_ref.shape[0]
    pairs = (
        (conc_ref, conc_in, 1),
        (pot_ref, pot_in, 0),
        (diff_ref, diff_in, 0),
        (spacer_ref, spacer_in, 0),
    )

    def empty_copy(slot):
        return pltpu.make_async_copy(empty, out_ref.at[slot], empty_sem.at[slot])

    def block_copy(chunk, part):
        return pltpu.make_async_copy(
            blocks.at[lax.rem(chunk, 2), part],
            out_ref.at[target_ref[chunk * BZ + part]],
            block_sem.at[lax.rem(chunk, 2), part],
        )

    @pl.when(step == 0)
    def _():
        for chunk in range(BX):
            for copy in load_copies(pairs, load_sem, chunk):
                copy.start()
        empty[...] = jnp.zeros_like(empty)

        @pl.loop(0, slots)
        def _(slot):
            @pl.when(filled_ref[slot] == 0)
            def _():
                empty_copy(slot).start()

        for plane, edge in ((0, xlo_ref), (NXL + 1, xhi_ref)):
            conc_in[0, plane] = edge[0]
            conc_in[1, plane] = edge[1]
            pot_in[plane] = edge[2]
            diff_in[plane] = edge[3]
            spacer_in[plane] = jnp.ones((NYL, NZL), jnp.int32)

    wait_chunks(step, pairs, load_sem)
    start = step * BLK

    def fields_of(first, second, pot, openness):
        root = openness * lax.rsqrt(jnp.maximum(openness, 1e-20))
        level = 0.5 * pot
        flux_first = root * first
        flux_second = root * second
        return (
            flux_first + level * flux_first,
            flux_first,
            flux_second - level * flux_second,
            flux_second,
            root,
            root * level,
        )

    @pl.loop(0, BLK + 2, unroll=2)
    def _(plane):
        at = start + plane
        openness = jnp.where(spacer_in[at] > 0, diff_in[at].astype(f32), 0.0)
        fields = fields_of(
            conc_in[0, at].astype(f32), conc_in[1, at].astype(f32), pot_in[at].astype(f32), openness
        )
        for number, field in enumerate(fields):
            wide[number, pl.ds(plane * ROWS + LOW, NYL), :] = field
            half[number, plane] = field.astype(bf16)

    for row, edge in ((LOW - 1, ylo_ref), (LOW + NYL, yhi_ref)):
        fields = fields_of(*[edge[number].astype(f32) for number in range(4)])
        for number, field in enumerate(fields):
            wide[number, pl.ds(ROWS + row, BLK, stride=ROWS), :] = field

    near = near_ref[...]

    @pl.loop(0, BLK // GROUP)
    def _(group):
        first = group * GROUP
        depth = []
        for number in range(6):
            centre = half[number, pl.ds(first + 1, GROUP)]
            sides = half[number, pl.ds(first, GROUP)] + half[number, pl.ds(first + 2, GROUP)]
            rows = jnp.concatenate([centre, sides], axis=2).reshape(GROUP * NYL, 2 * NZL)
            depth.append(jnp.dot(rows, near, preferred_element_type=f32))
        for plane in range(GROUP):
            base = (first + plane + 1) * ROWS + LOW
            total = []
            for number in range(6):
                total.append(
                    depth[number][plane * NYL : (plane + 1) * NYL]
                    + (
                        wide[number, pl.ds(base - 1, NYL), :]
                        + wide[number, pl.ds(base + 1, NYL), :]
                    )
                )
            at = start + first + plane + 1
            level = 0.5 * pot_in[at].astype(f32)
            root = ion_step * wide[4, pl.ds(base, NYL), :]
            tilt = level * total[4] - total[5]
            dens = conc_in[0, at].astype(f32)
            flux = total[0] - level * total[1] - dens * (total[4] + tilt)
            new_first = (dens + species_diff[0] * root * flux).astype(bf16)
            dens = conc_in[1, at].astype(f32)
            flux = total[2] + level * total[3] - dens * (total[4] - tilt)
            new_second = (dens + species_diff[1] * root * flux).astype(bf16)
            next_ref[0, first + plane] = new_first
            next_ref[1, first + plane] = new_second
            charge[pl.ds((first + plane) * NYL, NYL), :] = new_first.astype(f32) - new_second.astype(
                f32
            )

    for line in range(NYL // 4):
        for part in range(4):
            lines[pl.ds(line * BLK, BLK), pl.ds(part * NZL, NZL)] = charge[
                pl.ds(line * 4 + part, BLK, stride=NYL), :
            ].astype(bf16)

    @pl.when(step >= 2)
    def _():
        for part in range(BZ):
            block_copy(step - 2, part).wait()

    slot = lax.rem(step, 2)
    moved = jnp.dot(lines[...], order_ref[...], preferred_element_type=f32).astype(bf16)
    for line in range(NYL // 4):
        for part in range(BZ):
            blocks[slot, part, :, pl.ds(line * NZL, NZL)] = moved[
                line * BLK : (line + 1) * BLK, part * NZL : (part + 1) * NZL
            ]
    for part in range(BZ):
        block_copy(step, part).start()

    @pl.when(step == BX - 1)
    def _():
        for chunk in (BX - 2, BX - 1):
            for part in range(BZ):
                block_copy(chunk, part).wait()

        @pl.loop(0, slots)
        def _(slot):
            @pl.when(filled_ref[slot] == 0)
            def _():
                empty_copy(slot).wait()


def flow_kernel(
    vel_ref, pot_ref, spacer_ref, conc_ref, xlo_ref, xhi_ref, ylo_ref, yhi_ref, stencil_ref,
    out_ref,
    vel_in, pot_in, spacer_in, wide, half,
    load_sem,
):
    step = pl.program_id(0)
    pairs = ((vel_ref, vel_in, 1), (pot_ref, pot_in, 0), (spacer_ref, spacer_in, 0))

    @pl.when(step == 0)
    def _():
        for chunk in range(BX):
            for copy in load_copies(pairs, load_sem, chunk):
                copy.start()
        for plane, edge in ((0, xlo_ref), (NXL + 1, xhi_ref)):
            for number in range(3):
                vel_in[number, plane] = edge[number]
            pot_in[plane] = edge[3]
            spacer_in[plane] = jnp.ones((NYL, NZL), jnp.int32)

    wait_chunks(step, pairs, load_sem)
    start = step * BLK

    @pl.loop(0, BLK + 2, unroll=2)
    def _(plane):
        at = start + plane
        open_cells = spacer_in[at] > 0
        for number in range(3):
            field = jnp.where(open_cells, vel_in[number, at].astype(f32), 0.0)
            wide[number, pl.ds(plane * ROWS + LOW, NYL), :] = field
            half[number, plane] = field.astype(bf16)
        wide[3, pl.ds(plane * ROWS + LOW, NYL), :] = pot_in[at].astype(f32)

    for row, edge in ((LOW - 1, ylo_ref), (LOW + NYL, yhi_ref)):
        for number in range(4):
            wide[number, pl.ds(ROWS + row, BLK, stride=ROWS), :] = edge[number].astype(f32)

    stencil = stencil_ref[...]

    @pl.loop(0, BLK // GROUP)
    def _(group):
        first = group * GROUP
        depth = []
        for number in range(3):
            rows = half[number, pl.ds(first + 1, GROUP)].reshape(GROUP * NYL, NZL)
            depth.append(jnp.dot(rows, stencil, preferred_element_type=f32))
        rows = pot_in[pl.ds(start + first + 1, GROUP)].reshape(GROUP * NYL, NZL)
        pot_depth = jnp.dot(rows, stencil[:, NZL:], preferred_element_type=f32)
        for plane in range(GROUP):
            base = (first + plane + 1) * ROWS + LOW
            span = slice(plane * NYL, (plane + 1) * NYL)
            open_cells = spacer_in[start + first + plane + 1] > 0

            def near(number, offset):
                return wide[number, pl.ds(base + offset, NYL), :]

            charge = conc_ref[0, first + plane].astype(f32) - conc_ref[1, first + plane].astype(f32)
            centre = [near(number, 0) for number in range(3)]
            slopes = (
                near(3, ROWS) - near(3, -ROWS),
                near(3, 1) - near(3, -1),
                pot_depth[span],
            )
            for number in range(3):
                front, back = near(number, ROWS), near(number, -ROWS)
                right, left = near(number, 1), near(number, -1)
                total = (front + back) + (right + left) + depth[number][span, :NZL]
                carried = (
                    centre[0] * (front - back)
                    + centre[1] * (right - left)
                    + centre[2] * depth[number][span, NZL:]
                )
                value = (1.0 - 6.0 * flow_step * viscosity) * centre[number] + (
                    flow_step * viscosity
                ) * total - (0.5 * flow_step) * (carried + charge * slopes[number])
                out_ref[number, first + plane] = jnp.where(open_cells, value, 0.0).astype(bf16)


def any_spec():
    return pl.BlockSpec(memory_space=pl.ANY)


def whole_spec(shape):
    return pl.BlockSpec(shape, lambda step: (0,) * len(shape))


def run_ions(target, filled, concentration, potential, diffusivity, spacer, xlo, xhi, ylo, yhi):
    near = jnp.asarray(np.concatenate([near_sum_matrix(), np.eye(NZL, dtype=np.float32)]), bf16)
    order = jnp.asarray(block_order_matrix(), bf16)
    slots = filled.shape[0]
    plane = (NXL + 2, NYL, NZL)
    edge = pl.BlockSpec((4, BLK, NZL), lambda step: (0, step, 0))
    return pl.pallas_call(
        ion_kernel,
        grid=(BX,),
        in_specs=[
            pl.BlockSpec(memory_space=pltpu.SMEM),
            pl.BlockSpec(memory_space=pltpu.SMEM),
            any_spec(), any_spec(), any_spec(), any_spec(),
            whole_spec(xlo.shape), whole_spec(xhi.shape), edge, edge,
            whole_spec(near.shape), whole_spec(order.shape),
        ],
        out_specs=[
            pl.BlockSpec((2, BLK, NYL, NZL), lambda step: (0, step, 0, 0)),
            any_spec(),
        ],
        out_shape=[
            jax.ShapeDtypeStruct(concentration.shape, bf16),
            jax.ShapeDtypeStruct((slots, BLK, BLK * BLK), bf16),
        ],
        scratch_shapes=[
            pltpu.VMEM((2,) + plane, bf16),
            pltpu.VMEM(plane, bf16),
            pltpu.VMEM(plane, bf16),
            pltpu.VMEM(plane, jnp.int32),
            pltpu.VMEM((6, (BLK + 2) * ROWS, NZL), f32),
            pltpu.VMEM((6, BLK + 2, NYL, NZL), bf16),
            pltpu.VMEM((BLK * NYL, NZL), f32),
            pltpu.VMEM((NYL // 4 * BLK, 4 * NZL), bf16),
            pltpu.VMEM((2, BZ, BLK, BLK * BLK), bf16),
            pltpu.VMEM((BLK, BLK * BLK), bf16),
            pltpu.SemaphoreType.DMA((4, BX)),
            pltpu.SemaphoreType.DMA((2, BZ)),
            pltpu.SemaphoreType.DMA((slots,)),
        ],
        compiler_params=pltpu.CompilerParams(vmem_limit_bytes=48 * 1024 * 1024),
        cost_estimate=pl.CostEstimate(flops=200_000_000, bytes_accessed=17_000_000, transcendentals=0),
        name="ions",
    )(target, filled, concentration, potential, diffusivity, spacer, xlo, xhi, ylo, yhi, near, order)


def run_flow(velocity, potential, spacer, conc_next, xlo, xhi, ylo, yhi):
    stencil = jnp.asarray(np.concatenate([near_sum_matrix(), difference_matrix()], axis=1), bf16)
    plane = (NXL + 2, NYL, NZL)
    edge = pl.BlockSpec((4, BLK, NZL), lambda step: (0, step, 0))
    return pl.pallas_call(
        flow_kernel,
        grid=(BX,),
        in_specs=[
            any_spec(), any_spec(), any_spec(),
            pl.BlockSpec((2, BLK, NYL, NZL), lambda step: (0, step, 0, 0)),
            whole_spec(xlo.shape), whole_spec(xhi.shape), edge, edge,
            whole_spec(stencil.shape),
        ],
        out_specs=pl.BlockSpec((3, BLK, NYL, NZL), lambda step: (0, step, 0, 0)),
        out_shape=jax.ShapeDtypeStruct(velocity.shape, bf16),
        scratch_shapes=[
            pltpu.VMEM((3,) + plane, bf16),
            pltpu.VMEM(plane, bf16),
            pltpu.VMEM(plane, jnp.int32),
            pltpu.VMEM((4, (BLK + 2) * ROWS, NZL), f32),
            pltpu.VMEM((3, BLK + 2, NYL, NZL), bf16),
            pltpu.SemaphoreType.DMA((3, BX)),
        ],
        compiler_params=pltpu.CompilerParams(vmem_limit_bytes=48 * 1024 * 1024),
        cost_estimate=pl.CostEstimate(flops=200_000_000, bytes_accessed=17_000_000, transcendentals=0),
        name="flow",
    )(velocity, potential, spacer, conc_next, xlo, xhi, ylo, yhi, stencil)


def exchange(low_edge, high_edge, axis):
    count = lax.axis_size(axis)
    forward = [(i, (i + 1) % count) for i in range(count)]
    backward = [(i, (i - 1) % count) for i in range(count)]
    return lax.ppermute(high_edge, axis, forward), lax.ppermute(low_edge, axis, backward)


def per_device(concentration, potential, diffusivity, spacer, velocity, balance_plan):
    tiles = lax.axis_size("tile")
    count = balance_plan.shape[0]
    capacity = max(2, (2 * count + tiles - 1) // tiles)
    slots = tiles * capacity

    def cut(array, dim, index):
        return lax.index_in_dim(array, index, dim, keepdims=False)

    def edges_of(dim, index):
        solid = cut(spacer, dim, index) > 0
        conc = cut(concentration, dim + 1, index)
        pot = cut(potential, dim, index)[None]
        openness = jnp.where(solid, cut(diffusivity, dim, index), 0)[None]
        moving = jnp.where(solid[None], cut(velocity, dim + 1, index), 0)
        return jnp.concatenate([conc, pot, openness.astype(bf16)]), moving.astype(bf16)

    x_ion_low, x_flow_low = edges_of(0, 0)
    x_ion_high, x_flow_high = edges_of(0, NXL - 1)
    y_ion_low, y_flow_low = edges_of(1, 0)
    y_ion_high, y_flow_high = edges_of(1, NYL - 1)
    xlo, xhi = exchange(x_ion_low, x_ion_high, "stream")
    ylo, yhi = exchange(y_ion_low, y_ion_high, "tile")
    flow_xlo, flow_xhi = exchange(x_flow_low, x_flow_high, "stream")
    flow_ylo, flow_yhi = exchange(y_flow_low, y_flow_high, "tile")

    owners = balance_plan[:, 0]
    number = jnp.arange(count, dtype=jnp.int32)
    same_owner = owners[:, None] == owners[None, :]
    earlier = number[:, None] < number[None, :]
    ranking = jnp.sum(jnp.logical_and(same_owner, earlier).astype(jnp.int32), axis=0)
    target = owners * capacity + ranking
    filled = jnp.sum(
        (target[None, :] == jnp.arange(slots, dtype=jnp.int32)[:, None]).astype(jnp.int32), axis=1
    )

    conc_next, outgoing = run_ions(
        target, filled, concentration, potential, diffusivity, spacer, xlo, xhi, ylo, yhi
    )
    outgoing = outgoing.reshape(tiles, capacity, BLK, BLK * BLK)
    owned = lax.all_to_all(outgoing, "tile", split_axis=0, concat_axis=0, tiled=True)
    owned = owned.reshape(slots, BLK, BLK * BLK)

    def with_pot(flow, ion):
        return jnp.concatenate([flow, ion[2:3]])

    flow_next = run_flow(
        velocity, potential, spacer, conc_next,
        with_pot(flow_xlo, xlo), with_pot(flow_xhi, xhi),
        with_pot(flow_ylo, ylo), with_pot(flow_yhi, yhi),
    )
    return (conc_next, flow_next, owned)


def solution(mesh):
    placed = (
        P(None, "stream", "tile", None),
        P("stream", "tile", None),
        P("stream", "tile", None),
        P("stream", "tile", None),
        P(None, "stream", "tile", None),
        P(("stream", "tile"), None),
    )
    return jax.shard_map(
        per_device,
        mesh=mesh,
        in_specs=placed,
        out_specs=(
            P(None, "stream", "tile", None),
            P(None, "stream", "tile", None),
            P(("stream", "tile"), None, None),
        ),
        check_vma=False,
    )
```

```python
import jax
import jax.numpy as jnp
import numpy as np
from jax import lax
from jax.experimental import pallas as pl
from jax.experimental.pallas import tpu as pltpu
from jax.sharding import PartitionSpec as P

BLK = 32
BX = 6
BZ = 4
NXL = BX * BLK
NYL = BLK
NZL = BZ * BLK
ROWS = 48
LOW = 8
GROUP = 8
PART = 8

MESH = pl.DeviceIdType.MESH

ion_step = 0.04
flow_step = 0.1
viscosity = 0.5
species_diff = (1.0, 1.5)

f32 = jnp.float32
bf16 = jnp.bfloat16


def near_sum_matrix():
    line = np.arange(NZL)
    return (np.abs(line[:, None] - line[None, :]) == 1).astype(np.float32)


def difference_matrix():
    line = np.arange(NZL)
    step = line[:, None] - line[None, :]
    return (step == 1).astype(np.float32) - (step == -1).astype(np.float32)


def block_order_matrix():
    order = np.zeros((4 * NZL, 4 * NZL), np.float32)
    for part in range(4):
        for block in range(BZ):
            for cell in range(BLK):
                order[part * NZL + block * BLK + cell, block * NZL + part * BLK + cell] = 1
    return order


def load_copies(pairs, sem, chunk):
    span = pl.ds(chunk * BLK, BLK)
    inner = pl.ds(chunk * BLK + 1, BLK)
    copies = []
    for number, (source, target, lead) in enumerate(pairs):
        index_from = (slice(None),) * lead + (span,)
        index_to = (slice(None),) * lead + (inner,)
        copies.append(
            pltpu.make_async_copy(source.at[index_from], target.at[index_to], sem.at[number, chunk])
        )
    return copies


def wait_chunks(step, pairs, sem):
    @pl.when(step == 0)
    def _():
        for copy in load_copies(pairs, sem, 0):
            copy.wait()

    @pl.when(step < BX - 1)
    def _():
        for copy in load_copies(pairs, sem, step + 1):
            copy.wait()


def ion_kernel(
    source_ref, conc_ref, pot_ref, diff_ref, spacer_ref, vel_ref, near_ref, order_ref,
    next_ref, out_ref, yhalo_ref, xhalo_ref,
    conc_in, pot_in, diff_in, spacer_in, vel_in, vel_edge, edge_rows, y_send, y_recv, x_out,
    wide, half, charge, lines, blocks, staged, fresh,
    load_sem, vel_sem, xs_sem, xr_sem, ys_sem, yr_sem, fresh_sem, out_sem, halo_sem,
):
    slots = out_ref.shape[0]
    stream, tile = lax.axis_index("stream"), lax.axis_index("tile")
    streams, tiles = lax.axis_size("stream"), lax.axis_size("tile")
    x_near = (lax.rem(stream + streams - 1, streams), lax.rem(stream + 1, streams))
    y_near = (lax.rem(tile + tiles - 1, tiles), lax.rem(tile + 1, tiles))
    pairs = (
        (conc_ref, conc_in, 1),
        (pot_ref, pot_in, 0),
        (diff_ref, diff_in, 0),
        (spacer_ref, spacer_in, 0),
    )

    def vel_copy(chunk):
        span = pl.ds(chunk * BLK, BLK)
        return pltpu.make_async_copy(vel_ref.at[:, span], vel_in.at[:, span], vel_sem.at[chunk])

    def x_copies(side):
        edge = (0, NXL - 1)[side]
        halo = (NXL + 1, 0)[side]
        ends = (
            (conc_ref.at[:, edge], conc_in.at[:, halo]),
            (pot_ref.at[edge], pot_in.at[halo]),
            (diff_ref.at[edge], diff_in.at[halo]),
            (spacer_ref.at[edge], spacer_in.at[halo]),
            (vel_ref.at[:, edge], vel_edge.at[1 - side]),
        )
        return [
            pltpu.make_async_remote_copy(
                src_ref=source,
                dst_ref=target,
                send_sem=xs_sem.at[side, number],
                recv_sem=xr_sem.at[side, number],
                device_id=(x_near[side], tile),
                device_id_type=MESH,
            )
            for number, (source, target) in enumerate(ends)
        ]

    def y_copy(side, chunk):
        span = pl.ds(chunk * BLK, BLK)
        return pltpu.make_async_remote_copy(
            src_ref=y_send.at[side, :, span],
            dst_ref=y_recv.at[1 - side, :, span],
            send_sem=ys_sem.at[side, chunk],
            recv_sem=yr_sem.at[side, chunk],
            device_id=(stream, y_near[side]),
            device_id_type=MESH,
        )

    def fresh_copy(chunk):
        slot = lax.rem(chunk, 2)
        return pltpu.make_async_copy(
            fresh.at[slot], next_ref.at[:, pl.ds(chunk * BLK, BLK)], fresh_sem.at[slot]
        )

    def staged_copy(part):
        span = pl.ds(part * PART, PART)
        return pltpu.make_async_copy(staged.at[span], out_ref.at[span], out_sem.at[part])

    @pl.loop(0, BX)
    def _(chunk):
        for copy in load_copies(pairs, load_sem, chunk):
            copy.start()
        vel_copy(chunk).start()

    barrier = pltpu.get_barrier_semaphore()
    for near in x_near:
        pl.semaphore_signal(barrier, inc=1, device_id=(near, tile), device_id_type=MESH)
    for near in y_near:
        pl.semaphore_signal(barrier, inc=1, device_id=(stream, near), device_id_type=MESH)
    pl.semaphore_wait(barrier, 4)

    for side in range(2):
        for copy in x_copies(side):
            copy.start()

    blocks[BX * BZ] = jnp.zeros((BLK, BLK * BLK), bf16)

    @pl.loop(0, BX)
    def _(chunk):
        for copy in load_copies(pairs, load_sem, chunk):
            copy.wait()
        vel_copy(chunk).wait()

        @pl.loop(0, BLK, unroll=2)
        def _(plane):
            at = chunk * BLK + plane
            for side in range(2):
                rows = pl.ds(side * 16, 16)
                keep = slice(side * 8, side * 8 + 8)
                wet = spacer_in[at + 1, pl.ds(side * 24, 8), :] > 0
                put = pl.ds(plane * 8, 8)

                def part(ref, *index):
                    return ref[(*index, rows, slice(None))].astype(f32)[keep]

                edge_rows[side, 0, put, :] = part(conc_in, 0, at + 1)
                edge_rows[side, 1, put, :] = part(conc_in, 1, at + 1)
                edge_rows[side, 2, put, :] = jnp.where(wet, part(diff_in, at + 1), 0.0)
                edge_rows[side, 3, put, :] = part(pot_in, at + 1)
                for number in range(3):
                    edge_rows[side, 4 + number, put, :] = jnp.where(
                        wet, part(vel_in, number, at), 0.0
                    )

        for side in range(2):
            for number in range(7):
                y_send[side, number, pl.ds(chunk * BLK, BLK), :] = edge_rows[
                    side, number, pl.ds(side * 7, BLK, stride=8), :
                ].astype(bf16)
            y_copy(side, chunk).start()

    for side in range(2):
        for copy in x_copies(side):
            copy.wait_recv()

    for side, plane in ((0, 0), (1, NXL + 1)):
        wet = spacer_in[plane] > 0
        x_out[side, 3] = pot_in[plane]
        for number in range(3):
            x_out[side, number] = jnp.where(
                wet, vel_edge[side, number].astype(f32), 0.0
            ).astype(bf16)
    x_out_copy = pltpu.make_async_copy(x_out, xhalo_ref, halo_sem.at[0])
    x_out_copy.start()

    def fields_of(first, second, openness, pot):
        root = openness * lax.rsqrt(jnp.maximum(openness, 1e-20))
        level = 0.5 * pot
        flux_first = root * first
        flux_second = root * second
        return (
            flux_first + level * flux_first,
            flux_first,
            flux_second - level * flux_second,
            flux_second,
            root,
            root * level,
        )

    near = near_ref[...]

    @pl.loop(0, BX)
    def _(chunk):
        start = chunk * BLK

        @pl.loop(0, BLK + 2, unroll=2)
        def _(plane):
            at = start + plane
            openness = jnp.where(spacer_in[at] > 0, diff_in[at].astype(f32), 0.0)
            fields = fields_of(
                conc_in[0, at].astype(f32), conc_in[1, at].astype(f32), openness, pot_in[at].astype(f32)
            )
            for number, field in enumerate(fields):
                wide[number, pl.ds(plane * ROWS + LOW, NYL), :] = field
                half[number, plane] = field.astype(bf16)

        for side in range(2):
            y_copy(side, chunk).wait_recv()
        for side, row in ((0, LOW - 1), (1, LOW + NYL)):
            fields = fields_of(
                *[y_recv[side, number, pl.ds(start, BLK), :].astype(f32) for number in range(4)]
            )
            for number, field in enumerate(fields):
                wide[number, pl.ds(ROWS + row, BLK, stride=ROWS), :] = field

        @pl.when(chunk >= 2)
        def _():
            fresh_copy(chunk - 2).wait()

        slot = lax.rem(chunk, 2)

        @pl.loop(0, BLK // GROUP)
        def _(group):
            first = group * GROUP
            depth = []
            for number in range(6):
                centre = half[number, pl.ds(first + 1, GROUP)]
                sides = half[number, pl.ds(first, GROUP)] + half[number, pl.ds(first + 2, GROUP)]
                rows = jnp.concatenate([centre, sides], axis=2).reshape(GROUP * NYL, 2 * NZL)
                depth.append(jnp.dot(rows, near, preferred_element_type=f32))
            for plane in range(GROUP):
                base = (first + plane + 1) * ROWS + LOW
                total = []
                for number in range(6):
                    total.append(
                        depth[number][plane * NYL : (plane + 1) * NYL]
                        + (
                            wide[number, pl.ds(base - 1, NYL), :]
                            + wide[number, pl.ds(base + 1, NYL), :]
                        )
                    )
                at = start + first + plane + 1
                level = 0.5 * pot_in[at].astype(f32)
                root = ion_step * wide[4, pl.ds(base, NYL), :]
                tilt = level * total[4] - total[5]
                dens = conc_in[0, at].astype(f32)
                flux = total[0] - level * total[1] - dens * (total[4] + tilt)
                new_first = (dens + species_diff[0] * root * flux).astype(bf16)
                dens = conc_in[1, at].astype(f32)
                flux = total[2] + level * total[3] - dens * (total[4] - tilt)
                new_second = (dens + species_diff[1] * root * flux).astype(bf16)
                fresh[slot, 0, first + plane] = new_first
                fresh[slot, 1, first + plane] = new_second
                charge[pl.ds((first + plane) * NYL, NYL), :] = new_first.astype(
                    f32
                ) - new_second.astype(f32)

        fresh_copy(chunk).start()

        for line in range(NYL // 4):
            for part in range(4):
                lines[pl.ds(line * BLK, BLK), pl.ds(part * NZL, NZL)] = charge[
                    pl.ds(line * 4 + part, BLK, stride=NYL), :
                ].astype(bf16)
        moved = jnp.dot(lines[...], order_ref[...], preferred_element_type=f32).astype(bf16)
        for line in range(NYL // 4):
            for part in range(BZ):
                blocks[chunk * BZ + part, :, pl.ds(line * NZL, NZL)] = moved[
                    line * BLK : (line + 1) * BLK, part * NZL : (part + 1) * NZL
                ]

    y_out_copy = pltpu.make_async_copy(y_recv, yhalo_ref, halo_sem.at[1])
    y_out_copy.start()

    @pl.loop(0, slots // PART)
    def _(part):
        @pl.loop(0, PART)
        def _(number):
            staged[part * PART + number] = blocks[source_ref[part * PART + number]]

        staged_copy(part).start()

    for chunk in (BX - 2, BX - 1):
        fresh_copy(chunk).wait()
    x_out_copy.wait()
    y_out_copy.wait()
    for side in range(2):
        for copy in x_copies(side):
            copy.wait_send()

    @pl.loop(0, BX)
    def _(chunk):
        for side in range(2):
            y_copy(side, chunk).wait_send()

    @pl.loop(0, slots // PART)
    def _(part):
        staged_copy(part).wait()


def flow_kernel(
    vel_ref, pot_ref, spacer_ref, conc_ref, x_ref, y_ref, stencil_ref,
    out_ref, next_ref,
    vel_in, pot_in, spacer_in, wide, half,
    load_sem,
):
    step = pl.program_id(0)
    pairs = ((vel_ref, vel_in, 1), (pot_ref, pot_in, 0), (spacer_ref, spacer_in, 0))

    @pl.when(step == 0)
    def _():
        for chunk in range(BX):
            for copy in load_copies(pairs, load_sem, chunk):
                copy.start()
        for side, plane in ((0, 0), (1, NXL + 1)):
            for number in range(3):
                vel_in[number, plane] = x_ref[side, number]
            pot_in[plane] = x_ref[side, 3]
            spacer_in[plane] = jnp.ones((NYL, NZL), jnp.int32)

    wait_chunks(step, pairs, load_sem)
    start = step * BLK

    @pl.loop(0, BLK + 2, unroll=2)
    def _(plane):
        at = start + plane
        open_cells = spacer_in[at] > 0
        for number in range(3):
            field = jnp.where(open_cells, vel_in[number, at].astype(f32), 0.0)
            wide[number, pl.ds(plane * ROWS + LOW, NYL), :] = field
            half[number, plane] = field.astype(bf16)
        wide[3, pl.ds(plane * ROWS + LOW, NYL), :] = pot_in[at].astype(f32)

    next_ref[...] = conc_ref[...]

    for side, row in ((0, LOW - 1), (1, LOW + NYL)):
        for number, source in ((0, 4), (1, 5), (2, 6), (3, 3)):
            wide[number, pl.ds(ROWS + row, BLK, stride=ROWS), :] = y_ref[side, source].astype(f32)

    stencil = stencil_ref[...]

    @pl.loop(0, BLK // GROUP)
    def _(group):
        first = group * GROUP
        depth = []
        for number in range(3):
            rows = half[number, pl.ds(first + 1, GROUP)].reshape(GROUP * NYL, NZL)
            depth.append(jnp.dot(rows, stencil, preferred_element_type=f32))
        rows = pot_in[pl.ds(start + first + 1, GROUP)].reshape(GROUP * NYL, NZL)
        pot_depth = jnp.dot(rows, stencil[:, NZL:], preferred_element_type=f32)
        for plane in range(GROUP):
            base = (first + plane + 1) * ROWS + LOW
            span = slice(plane * NYL, (plane + 1) * NYL)
            open_cells = spacer_in[start + first + plane + 1] > 0

            def near(number, offset):
                return wide[number, pl.ds(base + offset, NYL), :]

            charge = conc_ref[0, first + plane].astype(f32) - conc_ref[1, first + plane].astype(f32)
            centre = [near(number, 0) for number in range(3)]
            slopes = (
                near(3, ROWS) - near(3, -ROWS),
                near(3, 1) - near(3, -1),
                pot_depth[span],
            )
            for number in range(3):
                front, back = near(number, ROWS), near(number, -ROWS)
                right, left = near(number, 1), near(number, -1)
                total = (front + back) + (right + left) + depth[number][span, :NZL]
                carried = (
                    centre[0] * (front - back)
                    + centre[1] * (right - left)
                    + centre[2] * depth[number][span, NZL:]
                )
                value = (1.0 - 6.0 * flow_step * viscosity) * centre[number] + (
                    flow_step * viscosity
                ) * total - (0.5 * flow_step) * (carried + charge * slopes[number])
                out_ref[number, first + plane] = jnp.where(open_cells, value, 0.0).astype(bf16)


def any_spec():
    return pl.BlockSpec(memory_space=pl.ANY)


def whole_spec(shape):
    return pl.BlockSpec(shape, lambda step: (0,) * len(shape))


def vmem_spec():
    return pl.BlockSpec(memory_space=pltpu.VMEM)


def run_ions(source, concentration, potential, diffusivity, spacer, velocity):
    near = jnp.asarray(np.concatenate([near_sum_matrix(), np.eye(NZL, dtype=np.float32)]), bf16)
    order = jnp.asarray(block_order_matrix(), bf16)
    slots = source.shape[0]
    plane = (NXL + 2, NYL, NZL)
    dma = pltpu.SemaphoreType.DMA
    return pl.pallas_call(
        ion_kernel,
        in_specs=[pl.BlockSpec(memory_space=pltpu.SMEM)] + [any_spec()] * 5 + [vmem_spec()] * 2,
        out_specs=[any_spec()] * 4,
        out_shape=[
            jax.ShapeDtypeStruct(concentration.shape, bf16),
            jax.ShapeDtypeStruct((slots, BLK, BLK * BLK), bf16),
            jax.ShapeDtypeStruct((2, 7, NXL, NZL), bf16),
            jax.ShapeDtypeStruct((2, 4, NYL, NZL), bf16),
        ],
        scratch_shapes=[
            pltpu.VMEM((2,) + plane, bf16),
            pltpu.VMEM(plane, bf16),
            pltpu.VMEM(plane, bf16),
            pltpu.VMEM(plane, jnp.int32),
            pltpu.VMEM(velocity.shape, bf16),
            pltpu.VMEM((2, 3, NYL, NZL), bf16),
            pltpu.VMEM((2, 7, BLK * 8, NZL), f32),
            pltpu.VMEM((2, 7, NXL, NZL), bf16),
            pltpu.VMEM((2, 7, NXL, NZL), bf16),
            pltpu.VMEM((2, 4, NYL, NZL), bf16),
            pltpu.VMEM((6, (BLK + 2) * ROWS, NZL), f32),
            pltpu.VMEM((6, BLK + 2, NYL, NZL), bf16),
            pltpu.VMEM((BLK * NYL, NZL), f32),
            pltpu.VMEM((NYL // 4 * BLK, 4 * NZL), bf16),
            pltpu.VMEM((BX * BZ + 1, BLK, BLK * BLK), bf16),
            pltpu.VMEM((slots, BLK, BLK * BLK), bf16),
            pltpu.VMEM((2, 2, BLK, NYL, NZL), bf16),
            dma((4, BX)),
            dma((BX,)),
            dma((2, 5)),
            dma((2, 5)),
            dma((2, BX)),
            dma((2, BX)),
            dma((2,)),
            dma((slots // PART,)),
            dma((2,)),
        ],
        compiler_params=pltpu.CompilerParams(
            vmem_limit_bytes=58 * 1024 * 1024, collective_id=0, has_side_effects=True
        ),
        cost_estimate=pl.CostEstimate(flops=200_000_000, bytes_accessed=17_000_000, transcendentals=0),
        name="ions",
    )(source, concentration, potential, diffusivity, spacer, velocity, near, order)


def run_flow(velocity, potential, spacer, conc_next, xhalo, yhalo):
    stencil = jnp.asarray(np.concatenate([near_sum_matrix(), difference_matrix()], axis=1), bf16)
    plane = (NXL + 2, NYL, NZL)
    return pl.pallas_call(
        flow_kernel,
        grid=(BX,),
        in_specs=[
            any_spec(), any_spec(), any_spec(),
            pl.BlockSpec((2, BLK, NYL, NZL), lambda step: (0, step, 0, 0)),
            whole_spec(xhalo.shape),
            pl.BlockSpec((2, 7, BLK, NZL), lambda step: (0, 0, step, 0)),
            whole_spec(stencil.shape),
        ],
        out_specs=[
            pl.BlockSpec((3, BLK, NYL, NZL), lambda step: (0, step, 0, 0)),
            pl.BlockSpec((2, BLK, NYL, NZL), lambda step: (0, step, 0, 0)),
        ],
        out_shape=[
            jax.ShapeDtypeStruct(velocity.shape, bf16),
            jax.ShapeDtypeStruct(conc_next.shape, bf16),
        ],
        scratch_shapes=[
            pltpu.VMEM((3,) + plane, bf16),
            pltpu.VMEM(plane, bf16),
            pltpu.VMEM(plane, jnp.int32),
            pltpu.VMEM((4, (BLK + 2) * ROWS, NZL), f32),
            pltpu.VMEM((3, BLK + 2, NYL, NZL), bf16),
            pltpu.SemaphoreType.DMA((3, BX)),
        ],
        compiler_params=pltpu.CompilerParams(vmem_limit_bytes=58 * 1024 * 1024),
        cost_estimate=pl.CostEstimate(flops=200_000_000, bytes_accessed=17_000_000, transcendentals=0),
        name="flow",
    )(velocity, potential, spacer, conc_next, xhalo, yhalo, stencil)


def per_device(concentration, potential, diffusivity, spacer, velocity, balance_plan):
    tiles = lax.axis_size("tile")
    count = balance_plan.shape[0]
    capacity = max(2, (2 * count + tiles - 1) // tiles)
    slots = tiles * capacity

    owners = balance_plan[:, 0]
    number = jnp.arange(count, dtype=jnp.int32)
    same_owner = owners[:, None] == owners[None, :]
    earlier = number[:, None] < number[None, :]
    ranking = jnp.sum(jnp.logical_and(same_owner, earlier).astype(jnp.int32), axis=0)
    target = owners * capacity + ranking
    named = target[None, :] == jnp.arange(slots, dtype=jnp.int32)[:, None]
    source = count + jnp.sum(jnp.where(named, number[None, :] - count, 0), axis=1)

    conc_next, outgoing, yhalo, xhalo = run_ions(
        source, concentration, potential, diffusivity, spacer, velocity
    )
    outgoing = outgoing.reshape(tiles, capacity, BLK, BLK * BLK)
    owned = lax.all_to_all(outgoing, "tile", split_axis=0, concat_axis=0, tiled=True)
    owned = owned.reshape(slots, BLK, BLK * BLK)

    flow_next, conc_next = run_flow(velocity, potential, spacer, conc_next, xhalo, yhalo)
    return (conc_next, flow_next, owned)


def solution(mesh):
    placed = (
        P(None, "stream", "tile", None),
        P("stream", "tile", None),
        P("stream", "tile", None),
        P("stream", "tile", None),
        P(None, "stream", "tile", None),
        P(("stream", "tile"), None),
    )
    return jax.shard_map(
        per_device,
        mesh=mesh,
        in_specs=placed,
        out_specs=(
            P(None, "stream", "tile", None),
            P(None, "stream", "tile", None),
            P(("stream", "tile"), None, None),
        ),
        check_vma=False,
    )
```

```python
import jax
import jax.numpy as jnp
import numpy as np
from jax import lax
from jax.experimental import pallas as pl
from jax.experimental.pallas import tpu as pltpu
from jax.sharding import PartitionSpec as P

BLK = 32
BX = 6
BZ = 4
NXL = BX * BLK
NYL = BLK
NZL = BZ * BLK
ROWS = 48
LOW = 8
GROUP = 32
PART = 8
COPIES = 16

MESH = pl.DeviceIdType.MESH

ion_step = 0.04
flow_step = 0.1
viscosity = 0.5
species_diff = (1.0, 1.5)

f32 = jnp.float32
bf16 = jnp.bfloat16


def near_sum_matrix():
    line = np.arange(NZL)
    return (np.abs(line[:, None] - line[None, :]) == 1).astype(np.float32)


def difference_matrix():
    line = np.arange(NZL)
    step = line[:, None] - line[None, :]
    return (step == 1).astype(np.float32) - (step == -1).astype(np.float32)


def block_order_matrix():
    order = np.zeros((4 * NZL, 4 * NZL), np.float32)
    for part in range(4):
        for block in range(BZ):
            for cell in range(BLK):
                order[part * NZL + block * BLK + cell, block * NZL + part * BLK + cell] = 1
    return order


def load_copies(pairs, sem, chunk):
    span = pl.ds(chunk * BLK, BLK)
    inner = pl.ds(chunk * BLK + 1, BLK)
    copies = []
    for number, (source, target, lead) in enumerate(pairs):
        index_from = (slice(None),) * lead + (span,)
        index_to = (slice(None),) * lead + (inner,)
        copies.append(
            pltpu.make_async_copy(source.at[index_from], target.at[index_to], sem.at[number, chunk])
        )
    return copies


def wait_chunks(step, pairs, sem):
    @pl.when(step == 0)
    def _():
        for copy in load_copies(pairs, sem, 0):
            copy.wait()

    @pl.when(step < BX - 1)
    def _():
        for copy in load_copies(pairs, sem, step + 1):
            copy.wait()


def ion_kernel(
    plan_ref, conc_ref, pot_ref, diff_ref, spacer_ref, vel_ref, near_ref, order_ref,
    next_ref, out_ref, yhalo_ref, xhalo_ref,
    conc_in, pot_in, diff_in, spacer_in, vel_in, vel_edge, edge_rows, y_send, y_recv, x_out,
    wide, half, charge, lines, blocks, staged, fresh, source_ref,
    load_sem, vel_sem, xs_sem, xr_sem, ys_sem, yr_sem, fresh_sem, out_sem, halo_sem,
):
    slots = out_ref.shape[0]
    stream, tile = lax.axis_index("stream"), lax.axis_index("tile")
    streams, tiles = lax.axis_size("stream"), lax.axis_size("tile")
    x_near = (lax.rem(stream + streams - 1, streams), lax.rem(stream + 1, streams))
    y_near = (lax.rem(tile + tiles - 1, tiles), lax.rem(tile + 1, tiles))
    pairs = (
        (conc_ref, conc_in, 1),
        (pot_ref, pot_in, 0),
        (diff_ref, diff_in, 0),
        (spacer_ref, spacer_in, 0),
    )

    def vel_copy(chunk):
        span = pl.ds(chunk * BLK, BLK)
        return pltpu.make_async_copy(vel_ref.at[:, span], vel_in.at[:, span], vel_sem.at[chunk])

    def x_copies(side):
        edge = (0, NXL - 1)[side]
        halo = (NXL + 1, 0)[side]
        ends = (
            (conc_ref.at[:, edge], conc_in.at[:, halo]),
            (pot_ref.at[edge], pot_in.at[halo]),
            (diff_ref.at[edge], diff_in.at[halo]),
            (spacer_ref.at[edge], spacer_in.at[halo]),
            (vel_ref.at[:, edge], vel_edge.at[1 - side]),
        )
        return [
            pltpu.make_async_remote_copy(
                src_ref=source,
                dst_ref=target,
                send_sem=xs_sem.at[side, number],
                recv_sem=xr_sem.at[side, number],
                device_id=(x_near[side], tile),
                device_id_type=MESH,
            )
            for number, (source, target) in enumerate(ends)
        ]

    def y_copy(side, chunk):
        span = pl.ds(chunk * BLK, BLK)
        return pltpu.make_async_remote_copy(
            src_ref=y_send.at[side, :, span],
            dst_ref=y_recv.at[1 - side, :, span],
            send_sem=ys_sem.at[side, chunk],
            recv_sem=yr_sem.at[side, chunk],
            device_id=(stream, y_near[side]),
            device_id_type=MESH,
        )

    def fresh_copy(chunk):
        slot = lax.rem(chunk, 2)
        return pltpu.make_async_copy(
            fresh.at[slot], next_ref.at[:, pl.ds(chunk * BLK, BLK)], fresh_sem.at[slot]
        )

    def staged_copy(part):
        span = pl.ds(part * PART, PART)
        return pltpu.make_async_copy(staged.at[span], out_ref.at[span], out_sem.at[part])

    @pl.loop(0, BX)
    def _(chunk):
        for copy in load_copies(pairs, load_sem, chunk):
            copy.start()
        vel_copy(chunk).start()

    barrier = pltpu.get_barrier_semaphore()
    for near in x_near:
        pl.semaphore_signal(barrier, inc=1, device_id=(near, tile), device_id_type=MESH)
    for near in y_near:
        pl.semaphore_signal(barrier, inc=1, device_id=(stream, near), device_id_type=MESH)

    @pl.loop(0, tiles)
    def _(owner):
        first = second = jnp.int32(BX * BZ)
        for block in reversed(range(BX * BZ)):
            named = plan_ref[block] == owner
            second = jnp.where(named, first, second)
            first = jnp.where(named, block, first)
        source_ref[2 * owner] = first
        source_ref[2 * owner + 1] = second

    pl.semaphore_wait(barrier, 4)

    for side in range(2):
        for copy in x_copies(side):
            copy.start()

    blocks[BX * BZ] = jnp.zeros((BLK, BLK * BLK), bf16)

    @pl.loop(0, BX)
    def _(chunk):
        for copy in load_copies(pairs, load_sem, chunk):
            copy.wait()
        vel_copy(chunk).wait()

        @pl.loop(0, BLK, unroll=8)
        def _(plane):
            at = chunk * BLK + plane
            for side in range(2):
                rows = pl.ds(side * 16, 16)
                keep = slice(side * 8, side * 8 + 8)
                wet = spacer_in[at + 1, pl.ds(side * 24, 8), :] > 0
                put = pl.ds(plane * 8, 8)

                def part(ref, *index):
                    return ref[(*index, rows, slice(None))].astype(f32)[keep]

                edge_rows[side, 0, put, :] = part(conc_in, 0, at + 1)
                edge_rows[side, 1, put, :] = part(conc_in, 1, at + 1)
                edge_rows[side, 2, put, :] = jnp.where(wet, part(diff_in, at + 1), 0.0)
                edge_rows[side, 3, put, :] = part(pot_in, at + 1)
                for number in range(3):
                    edge_rows[side, 4 + number, put, :] = jnp.where(
                        wet, part(vel_in, number, at), 0.0
                    )

        for side in range(2):
            for number in range(7):
                y_send[side, number, pl.ds(chunk * BLK, BLK), :] = edge_rows[
                    side, number, pl.ds(side * 7, BLK, stride=8), :
                ].astype(bf16)
            y_copy(side, chunk).start()

    for side in range(2):
        for copy in x_copies(side):
            copy.wait_recv()

    for side, plane in ((0, 0), (1, NXL + 1)):
        wet = spacer_in[plane] > 0
        x_out[side, 3] = pot_in[plane]
        for number in range(3):
            x_out[side, number] = jnp.where(
                wet, vel_edge[side, number].astype(f32), 0.0
            ).astype(bf16)
    x_out_copy = pltpu.make_async_copy(x_out, xhalo_ref, halo_sem.at[0])
    x_out_copy.start()

    def fields_of(first, second, openness, pot):
        root = openness * lax.rsqrt(jnp.maximum(openness, 1e-20))
        level = 0.5 * pot
        flux_first = root * first
        flux_second = root * second
        return (
            flux_first + level * flux_first,
            flux_first,
            flux_second - level * flux_second,
            flux_second,
            root,
            root * level,
        )

    near = near_ref[...]

    @pl.loop(0, BX)
    def _(chunk):
        start = chunk * BLK

        @pl.loop(0, BLK + 2, unroll=17)
        def _(plane):
            at = start + plane
            openness = jnp.where(spacer_in[at] > 0, diff_in[at].astype(f32), 0.0)
            fields = fields_of(
                conc_in[0, at].astype(f32), conc_in[1, at].astype(f32), openness, pot_in[at].astype(f32)
            )
            for number, field in enumerate(fields):
                wide[number, pl.ds(plane * ROWS + LOW, NYL), :] = field
                half[number, plane] = field.astype(bf16)

        for side in range(2):
            y_copy(side, chunk).wait_recv()
        for side, row in ((0, LOW - 1), (1, LOW + NYL)):
            fields = fields_of(
                *[y_recv[side, number, pl.ds(start, BLK), :].astype(f32) for number in range(4)]
            )
            for number, field in enumerate(fields):
                wide[number, pl.ds(ROWS + row, BLK, stride=ROWS), :] = field

        @pl.when(chunk >= 2)
        def _():
            fresh_copy(chunk - 2).wait()

        slot = lax.rem(chunk, 2)

        @pl.loop(0, BLK // GROUP)
        def _(group):
            first = group * GROUP
            depth = []
            for number in range(6):
                centre = half[number, pl.ds(first + 1, GROUP)]
                sides = half[number, pl.ds(first, GROUP)] + half[number, pl.ds(first + 2, GROUP)]
                rows = jnp.concatenate([centre, sides], axis=2).reshape(GROUP * NYL, 2 * NZL)
                depth.append(jnp.dot(rows, near, preferred_element_type=f32))
            for plane in range(GROUP):
                base = (first + plane + 1) * ROWS + LOW
                total = []
                for number in range(6):
                    total.append(
                        depth[number][plane * NYL : (plane + 1) * NYL]
                        + (
                            wide[number, pl.ds(base - 1, NYL), :]
                            + wide[number, pl.ds(base + 1, NYL), :]
                        )
                    )
                at = start + first + plane + 1
                level = 0.5 * pot_in[at].astype(f32)
                root = ion_step * wide[4, pl.ds(base, NYL), :]
                tilt = level * total[4] - total[5]
                dens = conc_in[0, at].astype(f32)
                flux = total[0] - level * total[1] - dens * (total[4] + tilt)
                new_first = (dens + species_diff[0] * root * flux).astype(bf16)
                dens = conc_in[1, at].astype(f32)
                flux = total[2] + level * total[3] - dens * (total[4] - tilt)
                new_second = (dens + species_diff[1] * root * flux).astype(bf16)
                fresh[slot, 0, first + plane] = new_first
                fresh[slot, 1, first + plane] = new_second
                charge[pl.ds((first + plane) * NYL, NYL), :] = new_first.astype(
                    f32
                ) - new_second.astype(f32)

        fresh_copy(chunk).start()

        for line in range(NYL // 4):
            for part in range(4):
                lines[pl.ds(line * BLK, BLK), pl.ds(part * NZL, NZL)] = charge[
                    pl.ds(line * 4 + part, BLK, stride=NYL), :
                ].astype(bf16)
        moved = jnp.dot(lines[...], order_ref[...], preferred_element_type=f32).astype(bf16)
        for line in range(NYL // 4):
            for part in range(BZ):
                blocks[chunk * BZ + part, :, pl.ds(line * NZL, NZL)] = moved[
                    line * BLK : (line + 1) * BLK, part * NZL : (part + 1) * NZL
                ]

    y_out_copy = pltpu.make_async_copy(y_recv, yhalo_ref, halo_sem.at[1])
    y_out_copy.start()

    @pl.loop(0, slots // PART)
    def _(part):
        @pl.loop(0, PART)
        def _(number):
            staged[part * PART + number] = blocks[source_ref[part * PART + number]]

        staged_copy(part).start()

    for chunk in (BX - 2, BX - 1):
        fresh_copy(chunk).wait()
    x_out_copy.wait()
    y_out_copy.wait()
    for side in range(2):
        for copy in x_copies(side):
            copy.wait_send()

    @pl.loop(0, BX)
    def _(chunk):
        for side in range(2):
            y_copy(side, chunk).wait_send()

    @pl.loop(0, slots // PART)
    def _(part):
        staged_copy(part).wait()


def flow_kernel(
    vel_ref, pot_ref, spacer_ref, conc_ref, x_ref, y_ref, stencil_ref,
    out_ref, next_ref,
    vel_in, pot_in, spacer_in, wide, half,
    load_sem,
):
    step = pl.program_id(0)
    pairs = ((vel_ref, vel_in, 1), (pot_ref, pot_in, 0), (spacer_ref, spacer_in, 0))

    @pl.when(step == 0)
    def _():
        for chunk in range(BX):
            for copy in load_copies(pairs, load_sem, chunk):
                copy.start()
        for side, plane in ((0, 0), (1, NXL + 1)):
            for number in range(3):
                vel_in[number, plane] = x_ref[side, number]
            pot_in[plane] = x_ref[side, 3]
            spacer_in[plane] = jnp.ones((NYL, NZL), jnp.int32)

    wait_chunks(step, pairs, load_sem)
    start = step * BLK

    @pl.loop(0, BLK + 2, unroll=17)
    def _(plane):
        at = start + plane
        open_cells = spacer_in[at] > 0
        for number in range(3):
            field = jnp.where(open_cells, vel_in[number, at].astype(f32), 0.0)
            wide[number, pl.ds(plane * ROWS + LOW, NYL), :] = field
            half[number, plane] = field.astype(bf16)
        wide[3, pl.ds(plane * ROWS + LOW, NYL), :] = pot_in[at].astype(f32)

    next_ref[...] = conc_ref[...]

    for side, row in ((0, LOW - 1), (1, LOW + NYL)):
        for number, source in ((0, 4), (1, 5), (2, 6), (3, 3)):
            wide[number, pl.ds(ROWS + row, BLK, stride=ROWS), :] = y_ref[side, source].astype(f32)

    stencil = stencil_ref[...]

    @pl.loop(0, BLK // GROUP)
    def _(group):
        first = group * GROUP
        depth = []
        for number in range(3):
            rows = half[number, pl.ds(first + 1, GROUP)].reshape(GROUP * NYL, NZL)
            depth.append(jnp.dot(rows, stencil, preferred_element_type=f32))
        rows = pot_in[pl.ds(start + first + 1, GROUP)].reshape(GROUP * NYL, NZL)
        pot_depth = jnp.dot(rows, stencil[:, NZL:], preferred_element_type=f32)
        for plane in range(GROUP):
            base = (first + plane + 1) * ROWS + LOW
            span = slice(plane * NYL, (plane + 1) * NYL)
            open_cells = spacer_in[start + first + plane + 1] > 0

            def near(number, offset):
                return wide[number, pl.ds(base + offset, NYL), :]

            charge = conc_ref[0, first + plane].astype(f32) - conc_ref[1, first + plane].astype(f32)
            centre = [near(number, 0) for number in range(3)]
            slopes = (
                near(3, ROWS) - near(3, -ROWS),
                near(3, 1) - near(3, -1),
                pot_depth[span],
            )
            for number in range(3):
                front, back = near(number, ROWS), near(number, -ROWS)
                right, left = near(number, 1), near(number, -1)
                total = (front + back) + (right + left) + depth[number][span, :NZL]
                carried = (
                    centre[0] * (front - back)
                    + centre[1] * (right - left)
                    + centre[2] * depth[number][span, NZL:]
                )
                value = (1.0 - 6.0 * flow_step * viscosity) * centre[number] + (
                    flow_step * viscosity
                ) * total - (0.5 * flow_step) * (carried + charge * slopes[number])
                out_ref[number, first + plane] = jnp.where(open_cells, value, 0.0).astype(bf16)


def any_spec():
    return pl.BlockSpec(memory_space=pl.ANY)


def whole_spec(shape):
    return pl.BlockSpec(shape, lambda step: (0,) * len(shape))


def vmem_spec():
    return pl.BlockSpec(memory_space=pltpu.VMEM)


def run_ions(plan, slots, concentration, potential, diffusivity, spacer, velocity):
    near = jnp.asarray(np.concatenate([near_sum_matrix(), np.eye(NZL, dtype=np.float32)]), bf16)
    order = jnp.asarray(block_order_matrix(), bf16)
    plane = (NXL + 2, NYL, NZL)
    dma = pltpu.SemaphoreType.DMA
    return pl.pallas_call(
        ion_kernel,
        in_specs=[pl.BlockSpec(memory_space=pltpu.SMEM)] + [any_spec()] * 5 + [vmem_spec()] * 2,
        out_specs=[any_spec()] * 4,
        out_shape=[
            jax.ShapeDtypeStruct(concentration.shape, bf16),
            jax.ShapeDtypeStruct((slots, BLK, BLK * BLK), bf16),
            jax.ShapeDtypeStruct((2, 7, NXL, NZL), bf16),
            jax.ShapeDtypeStruct((2, 4, NYL, NZL), bf16),
        ],
        scratch_shapes=[
            pltpu.VMEM((2,) + plane, bf16),
            pltpu.VMEM(plane, bf16),
            pltpu.VMEM(plane, bf16),
            pltpu.VMEM(plane, jnp.int32),
            pltpu.VMEM(velocity.shape, bf16),
            pltpu.VMEM((2, 3, NYL, NZL), bf16),
            pltpu.VMEM((2, 7, BLK * 8, NZL), f32),
            pltpu.VMEM((2, 7, NXL, NZL), bf16),
            pltpu.VMEM((2, 7, NXL, NZL), bf16),
            pltpu.VMEM((2, 4, NYL, NZL), bf16),
            pltpu.VMEM((6, (BLK + 2) * ROWS, NZL), f32),
            pltpu.VMEM((6, BLK + 2, NYL, NZL), bf16),
            pltpu.VMEM((BLK * NYL, NZL), f32),
            pltpu.VMEM((NYL // 4 * BLK, 4 * NZL), bf16),
            pltpu.VMEM((BX * BZ + 1, BLK, BLK * BLK), bf16),
            pltpu.VMEM((slots, BLK, BLK * BLK), bf16),
            pltpu.VMEM((2, 2, BLK, NYL, NZL), bf16),
            pltpu.SMEM((slots,), jnp.int32),
            dma((4, BX)),
            dma((BX,)),
            dma((2, 5)),
            dma((2, 5)),
            dma((2, BX)),
            dma((2, BX)),
            dma((2,)),
            dma((slots // PART,)),
            dma((2,)),
        ],
        compiler_params=pltpu.CompilerParams(
            vmem_limit_bytes=58 * 1024 * 1024, collective_id=0, has_side_effects=True
        ),
        cost_estimate=pl.CostEstimate(flops=200_000_000, bytes_accessed=17_000_000, transcendentals=0),
        name="ions",
    )(plan, concentration, potential, diffusivity, spacer, velocity, near, order)


def owned_kernel(part_ref, out_ref, held, in_sem, out_sem):
    size = held.shape[0] // COPIES

    def copy(number, source, target, sem):
        rows = pl.ds(number * size, size)
        return pltpu.make_async_copy(source.at[rows], target.at[rows], sem.at[number])

    for number in range(COPIES):
        copy(number, part_ref, held, in_sem).start()
    for number in range(COPIES):
        copy(number, part_ref, held, in_sem).wait()
        copy(number, held, out_ref, out_sem).start()
    for number in range(COPIES):
        copy(number, held, out_ref, out_sem).wait()


def put_owned(part):
    return pl.pallas_call(
        owned_kernel,
        in_specs=[any_spec()],
        out_specs=any_spec(),
        out_shape=jax.ShapeDtypeStruct(part.shape, bf16),
        scratch_shapes=[
            pltpu.VMEM(part.shape, bf16),
            pltpu.SemaphoreType.DMA((COPIES,)),
            pltpu.SemaphoreType.DMA((COPIES,)),
        ],
        compiler_params=pltpu.CompilerParams(vmem_limit_bytes=58 * 1024 * 1024),
        cost_estimate=pl.CostEstimate(flops=0, bytes_accessed=8_400_000, transcendentals=0),
        name="owned",
    )(part)


def run_flow(velocity, potential, spacer, conc_next, xhalo, yhalo):
    stencil = jnp.asarray(np.concatenate([near_sum_matrix(), difference_matrix()], axis=1), bf16)
    plane = (NXL + 2, NYL, NZL)
    return pl.pallas_call(
        flow_kernel,
        grid=(BX,),
        in_specs=[
            any_spec(), any_spec(), any_spec(),
            pl.BlockSpec((2, BLK, NYL, NZL), lambda step: (0, step, 0, 0)),
            whole_spec(xhalo.shape),
            pl.BlockSpec((2, 7, BLK, NZL), lambda step: (0, 0, step, 0)),
            whole_spec(stencil.shape),
        ],
        out_specs=[
            pl.BlockSpec((3, BLK, NYL, NZL), lambda step: (0, step, 0, 0)),
            pl.BlockSpec((2, BLK, NYL, NZL), lambda step: (0, step, 0, 0)),
        ],
        out_shape=[
            jax.ShapeDtypeStruct(velocity.shape, bf16),
            jax.ShapeDtypeStruct(conc_next.shape, bf16),
        ],
        scratch_shapes=[
            pltpu.VMEM((3,) + plane, bf16),
            pltpu.VMEM(plane, bf16),
            pltpu.VMEM(plane, jnp.int32),
            pltpu.VMEM((4, (BLK + 2) * ROWS, NZL), f32),
            pltpu.VMEM((3, BLK + 2, NYL, NZL), bf16),
            pltpu.SemaphoreType.DMA((3, BX)),
        ],
        compiler_params=pltpu.CompilerParams(vmem_limit_bytes=58 * 1024 * 1024),
        cost_estimate=pl.CostEstimate(flops=200_000_000, bytes_accessed=17_000_000, transcendentals=0),
        name="flow",
    )(velocity, potential, spacer, conc_next, xhalo, yhalo, stencil)


def per_device(concentration, potential, diffusivity, spacer, velocity, balance_plan):
    tiles = lax.axis_size("tile")
    capacity = 2
    slots = tiles * capacity
    conc_next, outgoing, yhalo, xhalo = run_ions(
        balance_plan[:, 0], slots, concentration, potential, diffusivity, spacer, velocity
    )
    outgoing = outgoing.reshape(tiles, capacity, BLK, BLK * BLK)
    owned = lax.all_to_all(outgoing, "tile", split_axis=0, concat_axis=0, tiled=True)
    owned = put_owned(owned.reshape(slots, BLK, BLK * BLK))

    flow_next, conc_next = run_flow(velocity, potential, spacer, conc_next, xhalo, yhalo)
    return (conc_next, flow_next, owned)


def solution(mesh):
    placed = (
        P(None, "stream", "tile", None),
        P("stream", "tile", None),
        P("stream", "tile", None),
        P("stream", "tile", None),
        P(None, "stream", "tile", None),
        P(("stream", "tile"), None),
    )
    return jax.shard_map(
        per_device,
        mesh=mesh,
        in_specs=placed,
        out_specs=(
            P(None, "stream", "tile", None),
            P(None, "stream", "tile", None),
            P(("stream", "tile"), None, None),
        ),
        check_vma=False,
    )
```

```python
import jax
import jax.numpy as jnp
import numpy as np
from jax import lax
from jax.experimental import pallas as pl
from jax.experimental.pallas import tpu as pltpu
from jax.sharding import PartitionSpec as P

BLK = 32
BX = 6
BZ = 4
NXL = BX * BLK
NYL = BLK
NZL = BZ * BLK
ROWS = 48
LOW = 8
GROUP = 32
PART = 8
COPIES = 16

MESH = pl.DeviceIdType.MESH

ion_step = 0.04
flow_step = 0.1
viscosity = 0.5
species_diff = (1.0, 1.5)

f32 = jnp.float32
bf16 = jnp.bfloat16


def near_sum_matrix():
    line = np.arange(NZL)
    return (np.abs(line[:, None] - line[None, :]) == 1).astype(np.float32)


def difference_matrix():
    line = np.arange(NZL)
    step = line[:, None] - line[None, :]
    return (step == 1).astype(np.float32) - (step == -1).astype(np.float32)


def block_order_matrix():
    order = np.zeros((4 * NZL, 4 * NZL), np.float32)
    for part in range(4):
        for block in range(BZ):
            for cell in range(BLK):
                order[part * NZL + block * BLK + cell, block * NZL + part * BLK + cell] = 1
    return order


def load_copies(pairs, sem, chunk):
    span = pl.ds(chunk * BLK, BLK)
    inner = pl.ds(chunk * BLK + 1, BLK)
    copies = []
    for number, (source, target, lead) in enumerate(pairs):
        index_from = (slice(None),) * lead + (span,)
        index_to = (slice(None),) * lead + (inner,)
        copies.append(
            pltpu.make_async_copy(source.at[index_from], target.at[index_to], sem.at[number, chunk])
        )
    return copies


def wait_chunks(step, pairs, sem):
    @pl.when(step == 0)
    def _():
        for copy in load_copies(pairs, sem, 0):
            copy.wait()

    @pl.when(step < BX - 1)
    def _():
        for copy in load_copies(pairs, sem, step + 1):
            copy.wait()


def ion_kernel(
    plan_ref, conc_ref, pot_ref, diff_ref, spacer_ref, vel_ref, near_ref, order_ref,
    next_ref, out_ref, yhalo_ref, xhalo_ref,
    conc_in, pot_in, diff_in, spacer_in, vel_in, vel_edge, edge_rows, y_send, y_recv, x_out,
    wide, half, charge, lines, blocks, staged, fresh, source_ref,
    load_sem, vel_sem, xs_sem, xr_sem, ys_sem, yr_sem, fresh_sem, out_sem, halo_sem,
):
    slots = out_ref.shape[0]
    stream, tile = lax.axis_index("stream"), lax.axis_index("tile")
    streams, tiles = lax.axis_size("stream"), lax.axis_size("tile")
    x_near = (lax.rem(stream + streams - 1, streams), lax.rem(stream + 1, streams))
    y_near = (lax.rem(tile + tiles - 1, tiles), lax.rem(tile + 1, tiles))
    pairs = (
        (conc_ref, conc_in, 1),
        (pot_ref, pot_in, 0),
        (diff_ref, diff_in, 0),
        (spacer_ref, spacer_in, 0),
    )

    def vel_copy(chunk):
        span = pl.ds(chunk * BLK, BLK)
        return pltpu.make_async_copy(vel_ref.at[:, span], vel_in.at[:, span], vel_sem.at[chunk])

    def x_copies(side):
        edge = (0, NXL - 1)[side]
        halo = (NXL + 1, 0)[side]
        ends = (
            (conc_ref.at[:, edge], conc_in.at[:, halo]),
            (pot_ref.at[edge], pot_in.at[halo]),
            (diff_ref.at[edge], diff_in.at[halo]),
            (spacer_ref.at[edge], spacer_in.at[halo]),
            (vel_ref.at[:, edge], vel_edge.at[1 - side]),
        )
        return [
            pltpu.make_async_remote_copy(
                src_ref=source,
                dst_ref=target,
                send_sem=xs_sem.at[side, number],
                recv_sem=xr_sem.at[side, number],
                device_id=(x_near[side], tile),
                device_id_type=MESH,
            )
            for number, (source, target) in enumerate(ends)
        ]

    def y_copy(side, chunk, kind):
        span = pl.ds(chunk * BLK, BLK)
        fields = (pl.ds(0, 4), pl.ds(4, 3))[kind]
        return pltpu.make_async_remote_copy(
            src_ref=y_send.at[side, fields, span],
            dst_ref=y_recv.at[1 - side, fields, span],
            send_sem=ys_sem.at[kind, side, chunk],
            recv_sem=yr_sem.at[kind, side, chunk],
            device_id=(stream, y_near[side]),
            device_id_type=MESH,
        )

    def fresh_copy(chunk):
        slot = lax.rem(chunk, 2)
        return pltpu.make_async_copy(
            fresh.at[slot], next_ref.at[:, pl.ds(chunk * BLK, BLK)], fresh_sem.at[slot]
        )

    def staged_copy(part):
        span = pl.ds(part * PART, PART)
        return pltpu.make_async_copy(staged.at[span], out_ref.at[span], out_sem.at[part])

    @pl.loop(0, BX)
    def _(chunk):
        for copy in load_copies(pairs, load_sem, chunk):
            copy.start()

    @pl.loop(0, BX)
    def _(chunk):
        vel_copy(chunk).start()

    barrier = pltpu.get_barrier_semaphore()
    for near in x_near:
        pl.semaphore_signal(barrier, inc=1, device_id=(near, tile), device_id_type=MESH)
    for near in y_near:
        pl.semaphore_signal(barrier, inc=1, device_id=(stream, near), device_id_type=MESH)

    @pl.loop(0, tiles)
    def _(owner):
        first = second = jnp.int32(BX * BZ)
        for block in reversed(range(BX * BZ)):
            named = plan_ref[block] == owner
            second = jnp.where(named, first, second)
            first = jnp.where(named, block, first)
        source_ref[2 * owner] = first
        source_ref[2 * owner + 1] = second

    pl.semaphore_wait(barrier, 4)

    for side in range(2):
        for copy in x_copies(side):
            copy.start()

    blocks[BX * BZ] = jnp.zeros((BLK, BLK * BLK), bf16)

    def pack_edges(chunk, kind):
        @pl.loop(0, BLK, unroll=8)
        def _(plane):
            at = chunk * BLK + plane
            for side in range(2):
                rows = pl.ds(side * 16, 16)
                keep = slice(side * 8, side * 8 + 8)
                wet = spacer_in[at + 1, pl.ds(side * 24, 8), :] > 0
                put = pl.ds(plane * 8, 8)

                def part(ref, *index):
                    return ref[(*index, rows, slice(None))].astype(f32)[keep]

                if kind == 0:
                    edge_rows[side, 0, put, :] = part(conc_in, 0, at + 1)
                    edge_rows[side, 1, put, :] = part(conc_in, 1, at + 1)
                    edge_rows[side, 2, put, :] = jnp.where(wet, part(diff_in, at + 1), 0.0)
                    edge_rows[side, 3, put, :] = part(pot_in, at + 1)
                else:
                    for number in range(3):
                        edge_rows[side, 4 + number, put, :] = jnp.where(
                            wet, part(vel_in, number, at), 0.0
                        )

        for side in range(2):
            for number in (range(4), range(4, 7))[kind]:
                y_send[side, number, pl.ds(chunk * BLK, BLK), :] = edge_rows[
                    side, number, pl.ds(side * 7, BLK, stride=8), :
                ].astype(bf16)
            y_copy(side, chunk, kind).start()

    @pl.loop(0, BX)
    def _(chunk):
        for copy in load_copies(pairs, load_sem, chunk):
            copy.wait()
        pack_edges(chunk, 0)

    for side in range(2):
        for copy in x_copies(side):
            copy.wait_recv()

    for side, plane in ((0, 0), (1, NXL + 1)):
        wet = spacer_in[plane] > 0
        x_out[side, 3] = pot_in[plane]
        for number in range(3):
            x_out[side, number] = jnp.where(
                wet, vel_edge[side, number].astype(f32), 0.0
            ).astype(bf16)
    x_out_copy = pltpu.make_async_copy(x_out, xhalo_ref, halo_sem.at[0])
    x_out_copy.start()

    def fields_of(first, second, openness, pot):
        root = openness * lax.rsqrt(jnp.maximum(openness, 1e-20))
        level = 0.5 * pot
        flux_first = root * first
        flux_second = root * second
        return (
            flux_first + level * flux_first,
            flux_first,
            flux_second - level * flux_second,
            flux_second,
            root,
            root * level,
        )

    near = near_ref[...]

    @pl.loop(0, BX)
    def _(chunk):
        start = chunk * BLK
        vel_copy(chunk).wait()
        pack_edges(chunk, 1)

        @pl.loop(0, BLK + 2, unroll=17)
        def _(plane):
            at = start + plane
            openness = jnp.where(spacer_in[at] > 0, diff_in[at].astype(f32), 0.0)
            fields = fields_of(
                conc_in[0, at].astype(f32), conc_in[1, at].astype(f32), openness, pot_in[at].astype(f32)
            )
            for number, field in enumerate(fields):
                wide[number, pl.ds(plane * ROWS + LOW, NYL), :] = field
                half[number, plane] = field.astype(bf16)

        for side in range(2):
            y_copy(side, chunk, 0).wait_recv()
        for side, row in ((0, LOW - 1), (1, LOW + NYL)):
            fields = fields_of(
                *[y_recv[side, number, pl.ds(start, BLK), :].astype(f32) for number in range(4)]
            )
            for number, field in enumerate(fields):
                wide[number, pl.ds(ROWS + row, BLK, stride=ROWS), :] = field

        @pl.when(chunk >= 2)
        def _():
            fresh_copy(chunk - 2).wait()

        slot = lax.rem(chunk, 2)

        @pl.loop(0, BLK // GROUP)
        def _(group):
            first = group * GROUP
            depth = []
            for number in range(6):
                centre = half[number, pl.ds(first + 1, GROUP)]
                sides = half[number, pl.ds(first, GROUP)] + half[number, pl.ds(first + 2, GROUP)]
                rows = jnp.concatenate([centre, sides], axis=2).reshape(GROUP * NYL, 2 * NZL)
                depth.append(jnp.dot(rows, near, preferred_element_type=f32))
            for plane in range(GROUP):
                base = (first + plane + 1) * ROWS + LOW
                total = []
                for number in range(6):
                    total.append(
                        depth[number][plane * NYL : (plane + 1) * NYL]
                        + (
                            wide[number, pl.ds(base - 1, NYL), :]
                            + wide[number, pl.ds(base + 1, NYL), :]
                        )
                    )
                at = start + first + plane + 1
                level = 0.5 * pot_in[at].astype(f32)
                root = ion_step * wide[4, pl.ds(base, NYL), :]
                tilt = level * total[4] - total[5]
                dens = conc_in[0, at].astype(f32)
                flux = total[0] - level * total[1] - dens * (total[4] + tilt)
                new_first = (dens + species_diff[0] * root * flux).astype(bf16)
                dens = conc_in[1, at].astype(f32)
                flux = total[2] + level * total[3] - dens * (total[4] - tilt)
                new_second = (dens + species_diff[1] * root * flux).astype(bf16)
                fresh[slot, 0, first + plane] = new_first
                fresh[slot, 1, first + plane] = new_second
                charge[pl.ds((first + plane) * NYL, NYL), :] = new_first.astype(
                    f32
                ) - new_second.astype(f32)

        fresh_copy(chunk).start()

        for line in range(NYL // 4):
            for part in range(4):
                lines[pl.ds(line * BLK, BLK), pl.ds(part * NZL, NZL)] = charge[
                    pl.ds(line * 4 + part, BLK, stride=NYL), :
                ].astype(bf16)
        moved = jnp.dot(lines[...], order_ref[...], preferred_element_type=f32).astype(bf16)
        for line in range(NYL // 4):
            for part in range(BZ):
                blocks[chunk * BZ + part, :, pl.ds(line * NZL, NZL)] = moved[
                    line * BLK : (line + 1) * BLK, part * NZL : (part + 1) * NZL
                ]

    @pl.loop(0, BX)
    def _(chunk):
        for side in range(2):
            y_copy(side, chunk, 1).wait_recv()

    y_out_copy = pltpu.make_async_copy(y_recv, yhalo_ref, halo_sem.at[1])
    y_out_copy.start()

    @pl.loop(0, slots // PART)
    def _(part):
        @pl.loop(0, PART)
        def _(number):
            staged[part * PART + number] = blocks[source_ref[part * PART + number]]

        staged_copy(part).start()

    for chunk in (BX - 2, BX - 1):
        fresh_copy(chunk).wait()
    x_out_copy.wait()
    y_out_copy.wait()
    for side in range(2):
        for copy in x_copies(side):
            copy.wait_send()

    @pl.loop(0, BX)
    def _(chunk):
        for side in range(2):
            for kind in range(2):
                y_copy(side, chunk, kind).wait_send()

    @pl.loop(0, slots // PART)
    def _(part):
        staged_copy(part).wait()


def flow_kernel(
    vel_ref, pot_ref, spacer_ref, conc_ref, x_ref, y_ref, stencil_ref,
    out_ref, next_ref,
    vel_in, pot_in, spacer_in, wide, half,
    load_sem,
):
    step = pl.program_id(0)
    pairs = ((vel_ref, vel_in, 1), (pot_ref, pot_in, 0), (spacer_ref, spacer_in, 0))

    @pl.when(step == 0)
    def _():
        for chunk in range(BX):
            for copy in load_copies(pairs, load_sem, chunk):
                copy.start()
        for side, plane in ((0, 0), (1, NXL + 1)):
            for number in range(3):
                vel_in[number, plane] = x_ref[side, number]
            pot_in[plane] = x_ref[side, 3]
            spacer_in[plane] = jnp.ones((NYL, NZL), jnp.int32)

    wait_chunks(step, pairs, load_sem)
    start = step * BLK

    @pl.loop(0, BLK + 2, unroll=17)
    def _(plane):
        at = start + plane
        open_cells = spacer_in[at] > 0
        for number in range(3):
            field = jnp.where(open_cells, vel_in[number, at].astype(f32), 0.0)
            wide[number, pl.ds(plane * ROWS + LOW, NYL), :] = field
            half[number, plane] = field.astype(bf16)
        wide[3, pl.ds(plane * ROWS + LOW, NYL), :] = pot_in[at].astype(f32)

    next_ref[...] = conc_ref[...]

    for side, row in ((0, LOW - 1), (1, LOW + NYL)):
        for number, source in ((0, 4), (1, 5), (2, 6), (3, 3)):
            wide[number, pl.ds(ROWS + row, BLK, stride=ROWS), :] = y_ref[side, source].astype(f32)

    stencil = stencil_ref[...]

    @pl.loop(0, BLK // GROUP)
    def _(group):
        first = group * GROUP
        depth = []
        for number in range(3):
            rows = half[number, pl.ds(first + 1, GROUP)].reshape(GROUP * NYL, NZL)
            depth.append(jnp.dot(rows, stencil, preferred_element_type=f32))
        rows = pot_in[pl.ds(start + first + 1, GROUP)].reshape(GROUP * NYL, NZL)
        pot_depth = jnp.dot(rows, stencil[:, NZL:], preferred_element_type=f32)
        for plane in range(GROUP):
            base = (first + plane + 1) * ROWS + LOW
            span = slice(plane * NYL, (plane + 1) * NYL)
            open_cells = spacer_in[start + first + plane + 1] > 0

            def near(number, offset):
                return wide[number, pl.ds(base + offset, NYL), :]

            charge = conc_ref[0, first + plane].astype(f32) - conc_ref[1, first + plane].astype(f32)
            centre = [near(number, 0) for number in range(3)]
            slopes = (
                near(3, ROWS) - near(3, -ROWS),
                near(3, 1) - near(3, -1),
                pot_depth[span],
            )
            for number in range(3):
                front, back = near(number, ROWS), near(number, -ROWS)
                right, left = near(number, 1), near(number, -1)
                total = (front + back) + (right + left) + depth[number][span, :NZL]
                carried = (
                    centre[0] * (front - back)
                    + centre[1] * (right - left)
                    + centre[2] * depth[number][span, NZL:]
                )
                value = (1.0 - 6.0 * flow_step * viscosity) * centre[number] + (
                    flow_step * viscosity
                ) * total - (0.5 * flow_step) * (carried + charge * slopes[number])
                out_ref[number, first + plane] = jnp.where(open_cells, value, 0.0).astype(bf16)


def any_spec():
    return pl.BlockSpec(memory_space=pl.ANY)


def whole_spec(shape):
    return pl.BlockSpec(shape, lambda step: (0,) * len(shape))


def vmem_spec():
    return pl.BlockSpec(memory_space=pltpu.VMEM)


def run_ions(plan, slots, concentration, potential, diffusivity, spacer, velocity):
    near = jnp.asarray(np.concatenate([near_sum_matrix(), np.eye(NZL, dtype=np.float32)]), bf16)
    order = jnp.asarray(block_order_matrix(), bf16)
    plane = (NXL + 2, NYL, NZL)
    dma = pltpu.SemaphoreType.DMA
    return pl.pallas_call(
        ion_kernel,
        in_specs=[pl.BlockSpec(memory_space=pltpu.SMEM)] + [any_spec()] * 5 + [vmem_spec()] * 2,
        out_specs=[any_spec()] * 4,
        out_shape=[
            jax.ShapeDtypeStruct(concentration.shape, bf16),
            jax.ShapeDtypeStruct((slots, BLK, BLK * BLK), bf16),
            jax.ShapeDtypeStruct((2, 7, NXL, NZL), bf16),
            jax.ShapeDtypeStruct((2, 4, NYL, NZL), bf16),
        ],
        scratch_shapes=[
            pltpu.VMEM((2,) + plane, bf16),
            pltpu.VMEM(plane, bf16),
            pltpu.VMEM(plane, bf16),
            pltpu.VMEM(plane, jnp.int32),
            pltpu.VMEM(velocity.shape, bf16),
            pltpu.VMEM((2, 3, NYL, NZL), bf16),
            pltpu.VMEM((2, 7, BLK * 8, NZL), f32),
            pltpu.VMEM((2, 7, NXL, NZL), bf16),
            pltpu.VMEM((2, 7, NXL, NZL), bf16),
            pltpu.VMEM((2, 4, NYL, NZL), bf16),
            pltpu.VMEM((6, (BLK + 2) * ROWS, NZL), f32),
            pltpu.VMEM((6, BLK + 2, NYL, NZL), bf16),
            pltpu.VMEM((BLK * NYL, NZL), f32),
            pltpu.VMEM((NYL // 4 * BLK, 4 * NZL), bf16),
            pltpu.VMEM((BX * BZ + 1, BLK, BLK * BLK), bf16),
            pltpu.VMEM((slots, BLK, BLK * BLK), bf16),
            pltpu.VMEM((2, 2, BLK, NYL, NZL), bf16),
            pltpu.SMEM((slots,), jnp.int32),
            dma((4, BX)),
            dma((BX,)),
            dma((2, 5)),
            dma((2, 5)),
            dma((2, 2, BX)),
            dma((2, 2, BX)),
            dma((2,)),
            dma((slots // PART,)),
            dma((2,)),
        ],
        compiler_params=pltpu.CompilerParams(
            vmem_limit_bytes=58 * 1024 * 1024, collective_id=0, has_side_effects=True
        ),
        cost_estimate=pl.CostEstimate(flops=200_000_000, bytes_accessed=17_000_000, transcendentals=0),
        name="ions",
    )(plan, concentration, potential, diffusivity, spacer, velocity, near, order)


def owned_kernel(part_ref, out_ref, held, in_sem, out_sem):
    size = held.shape[0] // COPIES

    def copy(number, source, target, sem):
        rows = pl.ds(number * size, size)
        return pltpu.make_async_copy(source.at[rows], target.at[rows], sem.at[number])

    for number in range(COPIES):
        copy(number, part_ref, held, in_sem).start()
    for number in range(COPIES):
        copy(number, part_ref, held, in_sem).wait()
        copy(number, held, out_ref, out_sem).start()
    for number in range(COPIES):
        copy(number, held, out_ref, out_sem).wait()


def put_owned(part):
    return pl.pallas_call(
        owned_kernel,
        in_specs=[any_spec()],
        out_specs=any_spec(),
        out_shape=jax.ShapeDtypeStruct(part.shape, bf16),
        scratch_shapes=[
            pltpu.VMEM(part.shape, bf16),
            pltpu.SemaphoreType.DMA((COPIES,)),
            pltpu.SemaphoreType.DMA((COPIES,)),
        ],
        compiler_params=pltpu.CompilerParams(vmem_limit_bytes=58 * 1024 * 1024),
        cost_estimate=pl.CostEstimate(flops=0, bytes_accessed=8_400_000, transcendentals=0),
        name="owned",
    )(part)


def run_flow(velocity, potential, spacer, conc_next, xhalo, yhalo):
    stencil = jnp.asarray(np.concatenate([near_sum_matrix(), difference_matrix()], axis=1), bf16)
    plane = (NXL + 2, NYL, NZL)
    return pl.pallas_call(
        flow_kernel,
        grid=(BX,),
        in_specs=[
            any_spec(), any_spec(), any_spec(),
            pl.BlockSpec((2, BLK, NYL, NZL), lambda step: (0, step, 0, 0)),
            whole_spec(xhalo.shape),
            pl.BlockSpec((2, 7, BLK, NZL), lambda step: (0, 0, step, 0)),
            whole_spec(stencil.shape),
        ],
        out_specs=[
            pl.BlockSpec((3, BLK, NYL, NZL), lambda step: (0, step, 0, 0)),
            pl.BlockSpec((2, BLK, NYL, NZL), lambda step: (0, step, 0, 0)),
        ],
        out_shape=[
            jax.ShapeDtypeStruct(velocity.shape, bf16),
            jax.ShapeDtypeStruct(conc_next.shape, bf16),
        ],
        scratch_shapes=[
            pltpu.VMEM((3,) + plane, bf16),
            pltpu.VMEM(plane, bf16),
            pltpu.VMEM(plane, jnp.int32),
            pltpu.VMEM((4, (BLK + 2) * ROWS, NZL), f32),
            pltpu.VMEM((3, BLK + 2, NYL, NZL), bf16),
            pltpu.SemaphoreType.DMA((3, BX)),
        ],
        compiler_params=pltpu.CompilerParams(vmem_limit_bytes=58 * 1024 * 1024),
        cost_estimate=pl.CostEstimate(flops=200_000_000, bytes_accessed=17_000_000, transcendentals=0),
        name="flow",
    )(velocity, potential, spacer, conc_next, xhalo, yhalo, stencil)


def per_device(concentration, potential, diffusivity, spacer, velocity, balance_plan):
    tiles = lax.axis_size("tile")
    capacity = 2
    slots = tiles * capacity
    conc_next, outgoing, yhalo, xhalo = run_ions(
        balance_plan[:, 0], slots, concentration, potential, diffusivity, spacer, velocity
    )
    outgoing = outgoing.reshape(tiles, capacity, BLK, BLK * BLK)
    owned = lax.all_to_all(outgoing, "tile", split_axis=0, concat_axis=0, tiled=True)
    owned = put_owned(owned.reshape(slots, BLK, BLK * BLK))

    flow_next, conc_next = run_flow(velocity, potential, spacer, conc_next, xhalo, yhalo)
    return (conc_next, flow_next, owned)


def solution(mesh):
    placed = (
        P(None, "stream", "tile", None),
        P("stream", "tile", None),
        P("stream", "tile", None),
        P("stream", "tile", None),
        P(None, "stream", "tile", None),
        P(("stream", "tile"), None),
    )
    return jax.shard_map(
        per_device,
        mesh=mesh,
        in_specs=placed,
        out_specs=(
            P(None, "stream", "tile", None),
            P(None, "stream", "tile", None),
            P(("stream", "tile"), None, None),
        ),
        check_vma=False,
    )
```

```python
import jax
import jax.numpy as jnp
import numpy as np
from jax import lax
from jax.experimental import pallas as pl
from jax.experimental.pallas import tpu as pltpu
from jax.sharding import PartitionSpec as P

BLK = 32
BX = 6
BZ = 4
NXL = BX * BLK
NYL = BLK
NZL = BZ * BLK
ROWS = 48
LOW = 8
GROUP = 32
PART = 8
COPIES = 16
PITCH = NYL + 1
EDGE_PITCH = 9

MESH = pl.DeviceIdType.MESH

ion_step = 0.04
flow_step = 0.1
viscosity = 0.5
species_diff = (1.0, 1.5)

f32 = jnp.float32
bf16 = jnp.bfloat16


def near_sum_matrix():
    line = np.arange(NZL)
    return (np.abs(line[:, None] - line[None, :]) == 1).astype(np.float32)


def difference_matrix():
    line = np.arange(NZL)
    step = line[:, None] - line[None, :]
    return (step == 1).astype(np.float32) - (step == -1).astype(np.float32)


def block_order_matrix():
    order = np.zeros((4 * NZL, 4 * NZL), np.float32)
    for part in range(4):
        for block in range(BZ):
            for cell in range(BLK):
                order[part * NZL + block * BLK + cell, block * NZL + part * BLK + cell] = 1
    return order


def load_copies(pairs, sem, chunk):
    span = pl.ds(chunk * BLK, BLK)
    inner = pl.ds(chunk * BLK + 1, BLK)
    copies = []
    for number, (source, target, lead) in enumerate(pairs):
        index_from = (slice(None),) * lead + (span,)
        index_to = (slice(None),) * lead + (inner,)
        copies.append(
            pltpu.make_async_copy(source.at[index_from], target.at[index_to], sem.at[number, chunk])
        )
    return copies


def wait_chunks(step, pairs, sem):
    @pl.when(step == 0)
    def _():
        for copy in load_copies(pairs, sem, 0):
            copy.wait()

    @pl.when(step < BX - 1)
    def _():
        for copy in load_copies(pairs, sem, step + 1):
            copy.wait()


def ion_kernel(
    plan_ref, conc_ref, pot_ref, diff_ref, spacer_ref, vel_ref, near_ref, order_ref,
    next_ref, out_ref, yhalo_ref, xhalo_ref,
    conc_in, pot_in, diff_in, spacer_in, vel_in, vel_edge, edge_rows, y_send, y_recv, x_out,
    wide, half, charge, lines, blocks, staged, fresh, source_ref,
    load_sem, vel_sem, xs_sem, xr_sem, ys_sem, yr_sem, fresh_sem, out_sem, halo_sem,
):
    slots = out_ref.shape[0]
    stream, tile = lax.axis_index("stream"), lax.axis_index("tile")
    streams, tiles = lax.axis_size("stream"), lax.axis_size("tile")
    x_near = (lax.rem(stream + streams - 1, streams), lax.rem(stream + 1, streams))
    y_near = (lax.rem(tile + tiles - 1, tiles), lax.rem(tile + 1, tiles))
    pairs = (
        (conc_ref, conc_in, 1),
        (pot_ref, pot_in, 0),
        (diff_ref, diff_in, 0),
        (spacer_ref, spacer_in, 0),
    )

    def vel_copy(chunk):
        span = pl.ds(chunk * BLK, BLK)
        return pltpu.make_async_copy(vel_ref.at[:, span], vel_in.at[:, span], vel_sem.at[chunk])

    def x_copies(side):
        edge = (0, NXL - 1)[side]
        halo = (NXL + 1, 0)[side]
        ends = (
            (conc_ref.at[:, edge], conc_in.at[:, halo]),
            (pot_ref.at[edge], pot_in.at[halo]),
            (diff_ref.at[edge], diff_in.at[halo]),
            (spacer_ref.at[edge], spacer_in.at[halo]),
            (vel_ref.at[:, edge], vel_edge.at[1 - side]),
        )
        return [
            pltpu.make_async_remote_copy(
                src_ref=source,
                dst_ref=target,
                send_sem=xs_sem.at[side, number],
                recv_sem=xr_sem.at[side, number],
                device_id=(x_near[side], tile),
                device_id_type=MESH,
            )
            for number, (source, target) in enumerate(ends)
        ]

    def y_copy(side, chunk):
        span = pl.ds(chunk * BLK, BLK)
        return pltpu.make_async_remote_copy(
            src_ref=y_send.at[side, :, span],
            dst_ref=y_recv.at[1 - side, :, span],
            send_sem=ys_sem.at[side, chunk],
            recv_sem=yr_sem.at[side, chunk],
            device_id=(stream, y_near[side]),
            device_id_type=MESH,
        )

    def fresh_copy(chunk):
        slot = lax.rem(chunk, 2)
        return pltpu.make_async_copy(
            fresh.at[slot], next_ref.at[:, pl.ds(chunk * BLK, BLK)], fresh_sem.at[slot]
        )

    def staged_copy(part):
        span = pl.ds(part * PART, PART)
        return pltpu.make_async_copy(staged.at[span], out_ref.at[span], out_sem.at[part])

    @pl.loop(0, BX)
    def _(chunk):
        for copy in load_copies(pairs, load_sem, chunk):
            copy.start()
        vel_copy(chunk).start()

    barrier = pltpu.get_barrier_semaphore()
    for near in x_near:
        pl.semaphore_signal(barrier, inc=1, device_id=(near, tile), device_id_type=MESH)
    for near in y_near:
        pl.semaphore_signal(barrier, inc=1, device_id=(stream, near), device_id_type=MESH)

    @pl.loop(0, tiles)
    def _(owner):
        first = second = jnp.int32(BX * BZ)
        for block in reversed(range(BX * BZ)):
            named = plan_ref[block] == owner
            second = jnp.where(named, first, second)
            first = jnp.where(named, block, first)
        source_ref[2 * owner] = first
        source_ref[2 * owner + 1] = second

    pl.semaphore_wait(barrier, 4)

    for side in range(2):
        for copy in x_copies(side):
            copy.start()

    blocks[BX * BZ] = jnp.zeros((BLK, BLK * BLK), bf16)

    @pl.loop(0, BX)
    def _(chunk):
        for copy in load_copies(pairs, load_sem, chunk):
            copy.wait()
        vel_copy(chunk).wait()

        @pl.loop(0, BLK, unroll=8)
        def _(plane):
            at = chunk * BLK + plane
            for side in range(2):
                rows = pl.ds(side * 16, 16)
                keep = slice(side * 8, side * 8 + 8)
                wet = spacer_in[at + 1, pl.ds(side * 24, 8), :] > 0
                put = pl.ds(plane * EDGE_PITCH, 8)

                def part(ref, *index):
                    return ref[(*index, rows, slice(None))].astype(f32)[keep]

                edge_rows[side, 0, put, :] = part(conc_in, 0, at + 1)
                edge_rows[side, 1, put, :] = part(conc_in, 1, at + 1)
                edge_rows[side, 2, put, :] = jnp.where(wet, part(diff_in, at + 1), 0.0)
                edge_rows[side, 3, put, :] = part(pot_in, at + 1)
                for number in range(3):
                    edge_rows[side, 4 + number, put, :] = jnp.where(
                        wet, part(vel_in, number, at), 0.0
                    )

        for side in range(2):
            for number in range(7):
                y_send[side, number, pl.ds(chunk * BLK, BLK), :] = edge_rows[
                    side, number, pl.ds(side * 7, BLK, stride=EDGE_PITCH), :
                ].astype(bf16)
            y_copy(side, chunk).start()

    for side in range(2):
        for copy in x_copies(side):
            copy.wait_recv()

    for side, plane in ((0, 0), (1, NXL + 1)):
        wet = spacer_in[plane] > 0
        x_out[side, 3] = pot_in[plane]
        for number in range(3):
            x_out[side, number] = jnp.where(
                wet, vel_edge[side, number].astype(f32), 0.0
            ).astype(bf16)
    x_out_copy = pltpu.make_async_copy(x_out, xhalo_ref, halo_sem.at[0])
    x_out_copy.start()

    def fields_of(first, second, openness, pot):
        root = openness * lax.rsqrt(jnp.maximum(openness, 1e-20))
        level = 0.5 * pot
        flux_first = root * first
        flux_second = root * second
        return (
            flux_first + level * flux_first,
            flux_first,
            flux_second - level * flux_second,
            flux_second,
            root,
            root * level,
        )

    near = near_ref[...]

    @pl.loop(0, BX)
    def _(chunk):
        start = chunk * BLK

        @pl.loop(0, BLK + 2, unroll=17)
        def _(plane):
            at = start + plane
            openness = jnp.where(spacer_in[at] > 0, diff_in[at].astype(f32), 0.0)
            fields = fields_of(
                conc_in[0, at].astype(f32), conc_in[1, at].astype(f32), openness, pot_in[at].astype(f32)
            )
            for number, field in enumerate(fields):
                wide[number, pl.ds(plane * ROWS + LOW, NYL), :] = field
                half[number, plane] = field.astype(bf16)

        for side in range(2):
            y_copy(side, chunk).wait_recv()
        for side, row in ((0, LOW - 1), (1, LOW + NYL)):
            fields = fields_of(
                *[y_recv[side, number, pl.ds(start, BLK), :].astype(f32) for number in range(4)]
            )
            for number, field in enumerate(fields):
                wide[number, pl.ds(ROWS + row, BLK, stride=ROWS), :] = field

        @pl.when(chunk >= 2)
        def _():
            fresh_copy(chunk - 2).wait()

        slot = lax.rem(chunk, 2)

        @pl.loop(0, BLK // GROUP)
        def _(group):
            first = group * GROUP
            depth = []
            for number in range(6):
                centre = half[number, pl.ds(first + 1, GROUP)]
                sides = half[number, pl.ds(first, GROUP)] + half[number, pl.ds(first + 2, GROUP)]
                rows = jnp.concatenate([centre, sides], axis=2).reshape(GROUP * NYL, 2 * NZL)
                depth.append(jnp.dot(rows, near, preferred_element_type=f32))
            for plane in range(GROUP):
                base = (first + plane + 1) * ROWS + LOW
                total = []
                for number in range(6):
                    total.append(
                        depth[number][plane * NYL : (plane + 1) * NYL]
                        + (
                            wide[number, pl.ds(base - 1, NYL), :]
                            + wide[number, pl.ds(base + 1, NYL), :]
                        )
                    )
                at = start + first + plane + 1
                level = 0.5 * pot_in[at].astype(f32)
                root = ion_step * wide[4, pl.ds(base, NYL), :]
                tilt = level * total[4] - total[5]
                dens = conc_in[0, at].astype(f32)
                flux = total[0] - level * total[1] - dens * (total[4] + tilt)
                new_first = (dens + species_diff[0] * root * flux).astype(bf16)
                dens = conc_in[1, at].astype(f32)
                flux = total[2] + level * total[3] - dens * (total[4] - tilt)
                new_second = (dens + species_diff[1] * root * flux).astype(bf16)
                fresh[slot, 0, first + plane] = new_first
                fresh[slot, 1, first + plane] = new_second
                charge[pl.ds((first + plane) * PITCH, NYL), :] = new_first.astype(
                    f32
                ) - new_second.astype(f32)

        fresh_copy(chunk).start()

        for line in range(NYL // 4):
            for part in range(4):
                lines[pl.ds(line * BLK, BLK), pl.ds(part * NZL, NZL)] = charge[
                    pl.ds(line * 4 + part, BLK, stride=PITCH), :
                ].astype(bf16)
        moved = jnp.dot(lines[...], order_ref[...], preferred_element_type=f32).astype(bf16)
        for line in range(NYL // 4):
            for part in range(BZ):
                blocks[chunk * BZ + part, :, pl.ds(line * NZL, NZL)] = moved[
                    line * BLK : (line + 1) * BLK, part * NZL : (part + 1) * NZL
                ]

    y_out_copy = pltpu.make_async_copy(y_recv, yhalo_ref, halo_sem.at[1])
    y_out_copy.start()

    @pl.loop(0, slots // PART)
    def _(part):
        @pl.loop(0, PART)
        def _(number):
            staged[part * PART + number] = blocks[source_ref[part * PART + number]]

        staged_copy(part).start()

    for chunk in (BX - 2, BX - 1):
        fresh_copy(chunk).wait()
    x_out_copy.wait()
    y_out_copy.wait()
    for side in range(2):
        for copy in x_copies(side):
            copy.wait_send()

    @pl.loop(0, BX)
    def _(chunk):
        for side in range(2):
            y_copy(side, chunk).wait_send()

    @pl.loop(0, slots // PART)
    def _(part):
        staged_copy(part).wait()


def flow_kernel(
    vel_ref, pot_ref, spacer_ref, conc_ref, x_ref, y_ref, stencil_ref,
    out_ref, next_ref,
    vel_in, pot_in, spacer_in, wide, half,
    load_sem,
):
    step = pl.program_id(0)
    pairs = ((vel_ref, vel_in, 1), (pot_ref, pot_in, 0), (spacer_ref, spacer_in, 0))

    @pl.when(step == 0)
    def _():
        for chunk in range(BX):
            for copy in load_copies(pairs, load_sem, chunk):
                copy.start()
        for side, plane in ((0, 0), (1, NXL + 1)):
            for number in range(3):
                vel_in[number, plane] = x_ref[side, number]
            pot_in[plane] = x_ref[side, 3]
            spacer_in[plane] = jnp.ones((NYL, NZL), jnp.int32)

    wait_chunks(step, pairs, load_sem)
    start = step * BLK

    @pl.loop(0, BLK + 2, unroll=17)
    def _(plane):
        at = start + plane
        open_cells = spacer_in[at] > 0
        for number in range(3):
            field = jnp.where(open_cells, vel_in[number, at].astype(f32), 0.0)
            wide[number, pl.ds(plane * ROWS + LOW, NYL), :] = field
            half[number, plane] = field.astype(bf16)
        wide[3, pl.ds(plane * ROWS + LOW, NYL), :] = pot_in[at].astype(f32)

    next_ref[...] = conc_ref[...]

    for side, row in ((0, LOW - 1), (1, LOW + NYL)):
        for number, source in ((0, 4), (1, 5), (2, 6), (3, 3)):
            wide[number, pl.ds(ROWS + row, BLK, stride=ROWS), :] = y_ref[side, source].astype(f32)

    stencil = stencil_ref[...]

    @pl.loop(0, BLK // GROUP)
    def _(group):
        first = group * GROUP
        depth = []
        for number in range(3):
            rows = half[number, pl.ds(first + 1, GROUP)].reshape(GROUP * NYL, NZL)
            depth.append(jnp.dot(rows, stencil, preferred_element_type=f32))
        rows = pot_in[pl.ds(start + first + 1, GROUP)].reshape(GROUP * NYL, NZL)
        pot_depth = jnp.dot(rows, stencil[:, NZL:], preferred_element_type=f32)
        for plane in range(GROUP):
            base = (first + plane + 1) * ROWS + LOW
            span = slice(plane * NYL, (plane + 1) * NYL)
            open_cells = spacer_in[start + first + plane + 1] > 0

            def near(number, offset):
                return wide[number, pl.ds(base + offset, NYL), :]

            charge = conc_ref[0, first + plane].astype(f32) - conc_ref[1, first + plane].astype(f32)
            centre = [near(number, 0) for number in range(3)]
            slopes = (
                near(3, ROWS) - near(3, -ROWS),
                near(3, 1) - near(3, -1),
                pot_depth[span],
            )
            for number in range(3):
                front, back = near(number, ROWS), near(number, -ROWS)
                right, left = near(number, 1), near(number, -1)
                total = (front + back) + (right + left) + depth[number][span, :NZL]
                carried = (
                    centre[0] * (front - back)
                    + centre[1] * (right - left)
                    + centre[2] * depth[number][span, NZL:]
                )
                value = (1.0 - 6.0 * flow_step * viscosity) * centre[number] + (
                    flow_step * viscosity
                ) * total - (0.5 * flow_step) * (carried + charge * slopes[number])
                out_ref[number, first + plane] = jnp.where(open_cells, value, 0.0).astype(bf16)


def any_spec():
    return pl.BlockSpec(memory_space=pl.ANY)


def whole_spec(shape):
    return pl.BlockSpec(shape, lambda step: (0,) * len(shape))


def vmem_spec():
    return pl.BlockSpec(memory_space=pltpu.VMEM)


def run_ions(plan, slots, concentration, potential, diffusivity, spacer, velocity):
    near = jnp.asarray(np.concatenate([near_sum_matrix(), np.eye(NZL, dtype=np.float32)]), bf16)
    order = jnp.asarray(block_order_matrix(), bf16)
    plane = (NXL + 2, NYL, NZL)
    dma = pltpu.SemaphoreType.DMA
    return pl.pallas_call(
        ion_kernel,
        in_specs=[pl.BlockSpec(memory_space=pltpu.SMEM)] + [any_spec()] * 5 + [vmem_spec()] * 2,
        out_specs=[any_spec()] * 4,
        out_shape=[
            jax.ShapeDtypeStruct(concentration.shape, bf16),
            jax.ShapeDtypeStruct((slots, BLK, BLK * BLK), bf16),
            jax.ShapeDtypeStruct((2, 7, NXL, NZL), bf16),
            jax.ShapeDtypeStruct((2, 4, NYL, NZL), bf16),
        ],
        scratch_shapes=[
            pltpu.VMEM((2,) + plane, bf16),
            pltpu.VMEM(plane, bf16),
            pltpu.VMEM(plane, bf16),
            pltpu.VMEM(plane, jnp.int32),
            pltpu.VMEM(velocity.shape, bf16),
            pltpu.VMEM((2, 3, NYL, NZL), bf16),
            pltpu.VMEM((2, 7, BLK * EDGE_PITCH, NZL), f32),
            pltpu.VMEM((2, 7, NXL, NZL), bf16),
            pltpu.VMEM((2, 7, NXL, NZL), bf16),
            pltpu.VMEM((2, 4, NYL, NZL), bf16),
            pltpu.VMEM((6, (BLK + 2) * ROWS, NZL), f32),
            pltpu.VMEM((6, BLK + 2, NYL, NZL), bf16),
            pltpu.VMEM((BLK * PITCH, NZL), f32),
            pltpu.VMEM((NYL // 4 * BLK, 4 * NZL), bf16),
            pltpu.VMEM((BX * BZ + 1, BLK, BLK * BLK), bf16),
            pltpu.VMEM((slots, BLK, BLK * BLK), bf16),
            pltpu.VMEM((2, 2, BLK, NYL, NZL), bf16),
            pltpu.SMEM((slots,), jnp.int32),
            dma((4, BX)),
            dma((BX,)),
            dma((2, 5)),
            dma((2, 5)),
            dma((2, BX)),
            dma((2, BX)),
            dma((2,)),
            dma((slots // PART,)),
            dma((2,)),
        ],
        compiler_params=pltpu.CompilerParams(
            vmem_limit_bytes=58 * 1024 * 1024, collective_id=0, has_side_effects=True
        ),
        cost_estimate=pl.CostEstimate(flops=200_000_000, bytes_accessed=17_000_000, transcendentals=0),
        name="ions",
    )(plan, concentration, potential, diffusivity, spacer, velocity, near, order)


def owned_kernel(part_ref, out_ref, held, in_sem, out_sem):
    size = held.shape[0] // COPIES

    def copy(number, source, target, sem):
        rows = pl.ds(number * size, size)
        return pltpu.make_async_copy(source.at[rows], target.at[rows], sem.at[number])

    for number in range(COPIES):
        copy(number, part_ref, held, in_sem).start()
    for number in range(COPIES):
        copy(number, part_ref, held, in_sem).wait()
        copy(number, held, out_ref, out_sem).start()
    for number in range(COPIES):
        copy(number, held, out_ref, out_sem).wait()


def put_owned(part):
    return pl.pallas_call(
        owned_kernel,
        in_specs=[any_spec()],
        out_specs=any_spec(),
        out_shape=jax.ShapeDtypeStruct(part.shape, bf16),
        scratch_shapes=[
            pltpu.VMEM(part.shape, bf16),
            pltpu.SemaphoreType.DMA((COPIES,)),
            pltpu.SemaphoreType.DMA((COPIES,)),
        ],
        compiler_params=pltpu.CompilerParams(vmem_limit_bytes=58 * 1024 * 1024),
        cost_estimate=pl.CostEstimate(flops=0, bytes_accessed=8_400_000, transcendentals=0),
        name="owned",
    )(part)


def run_flow(velocity, potential, spacer, conc_next, xhalo, yhalo):
    stencil = jnp.asarray(np.concatenate([near_sum_matrix(), difference_matrix()], axis=1), bf16)
    plane = (NXL + 2, NYL, NZL)
    return pl.pallas_call(
        flow_kernel,
        grid=(BX,),
        in_specs=[
            any_spec(), any_spec(), any_spec(),
            pl.BlockSpec((2, BLK, NYL, NZL), lambda step: (0, step, 0, 0)),
            whole_spec(xhalo.shape),
            pl.BlockSpec((2, 7, BLK, NZL), lambda step: (0, 0, step, 0)),
            whole_spec(stencil.shape),
        ],
        out_specs=[
            pl.BlockSpec((3, BLK, NYL, NZL), lambda step: (0, step, 0, 0)),
            pl.BlockSpec((2, BLK, NYL, NZL), lambda step: (0, step, 0, 0)),
        ],
        out_shape=[
            jax.ShapeDtypeStruct(velocity.shape, bf16),
            jax.ShapeDtypeStruct(conc_next.shape, bf16),
        ],
        scratch_shapes=[
            pltpu.VMEM((3,) + plane, bf16),
            pltpu.VMEM(plane, bf16),
            pltpu.VMEM(plane, jnp.int32),
            pltpu.VMEM((4, (BLK + 2) * ROWS, NZL), f32),
            pltpu.VMEM((3, BLK + 2, NYL, NZL), bf16),
            pltpu.SemaphoreType.DMA((3, BX)),
        ],
        compiler_params=pltpu.CompilerParams(vmem_limit_bytes=58 * 1024 * 1024),
        cost_estimate=pl.CostEstimate(flops=200_000_000, bytes_accessed=17_000_000, transcendentals=0),
        name="flow",
    )(velocity, potential, spacer, conc_next, xhalo, yhalo, stencil)


def per_device(concentration, potential, diffusivity, spacer, velocity, balance_plan):
    tiles = lax.axis_size("tile")
    capacity = 2
    slots = tiles * capacity
    conc_next, outgoing, yhalo, xhalo = run_ions(
        balance_plan[:, 0], slots, concentration, potential, diffusivity, spacer, velocity
    )
    outgoing = outgoing.reshape(tiles, capacity, BLK, BLK * BLK)
    owned = lax.all_to_all(outgoing, "tile", split_axis=0, concat_axis=0, tiled=True)
    owned = put_owned(owned.reshape(slots, BLK, BLK * BLK))

    flow_next, conc_next = run_flow(velocity, potential, spacer, conc_next, xhalo, yhalo)
    return (conc_next, flow_next, owned)


def solution(mesh):
    placed = (
        P(None, "stream", "tile", None),
        P("stream", "tile", None),
        P("stream", "tile", None),
        P("stream", "tile", None),
        P(None, "stream", "tile", None),
        P(("stream", "tile"), None),
    )
    return jax.shard_map(
        per_device,
        mesh=mesh,
        in_specs=placed,
        out_specs=(
            P(None, "stream", "tile", None),
            P(None, "stream", "tile", None),
            P(("stream", "tile"), None, None),
        ),
        check_vma=False,
    )
```
